256 devices in a mesh: dp: 2 (over core), row: 32 (over x, z), dim: 4 (over y).
Axes of the slice: x: 4, y: 4, z: 8, core: 2. Of those that a mesh axis runs over, the one named last changes fastest.
Arguments:
- tokens: bfloat16 [8192, 2048], P(('dp', 'row'), 'dim'), may hold values from -6 to 6
- query_weight: bfloat16 [2048, 512], P('dim'), may hold values from -0.125 to 0.125
- keys_first: bfloat16 [64, 256], replicated, may hold values from -0.375 to 0.375
- keys_second: bfloat16 [1024, 256], replicated, may hold values from -0.375 to 0.375
- values: bfloat16 [65536, 1024], P('row', 'dim'), may hold values from -6 to 6
- picks: int32 [8192, 32], P(('dp', 'row')), may hold values from 0 to 65535, as said below
- out_grad: bfloat16 [8192, 1024], P(('dp', 'row'), 'dim'), may hold values from -6 to 6
Outputs:
- mixed: bfloat16 [8192, 1024], P(('dp', 'row'), 'dim')
- token_grad: bfloat16 [8192, 2048], P(('dp', 'row'), 'dim')
- query_weight_grad: float32 [2048, 512], P('dim')
- first_key_grad: float32 [64, 256], replicated
- second_key_grad: float32 [1024, 256], replicated
- value_grad: float32 [65536, 1024], P(('row', 'dp'), 'dim')
The draws below stay inside these ranges and needn't reach their ends.
Inputs may be any that keep to these rules, and one draw needn't show every extreme that they name: Call rows k * 2048 to (k + 1) * 2048 - 1 owner k's rows. Of the picks of one device's 128 tokens (aligned blocks of 128 token rows), at most 256 fall on one owner's rows; one owner, the same for every block, receives exactly 256 picks from every block.
All inputs are finite; a program needn't handle non-finite values.
Results may differ from the reference program's by a relative error of at most 0.0065.
Values may be sent and summed in bfloat16 or wider, within the bound.
No kernel may reach another device: no remote copies, remote signals or barrier semaphores. Data moves between devices by JAX's collectives and lax.ppermute only.
A program may use at most 64 MiB of HBM per device.

```python
import math
import jax
import jax.numpy as jnp
from jax import lax

D = 2048
VD = 1024
KD = 512
NB = 1024
TOPK = 32
TOK_DEV = 128
ROW_DEV = 2048
H = 256
TOKENS = 8192
ROWS = 65536
NA = 64
CAP = 256


def draw_picks(key, part):
    key = jax.random.fold_in(key, 11)
    owners_count = ROWS // ROW_DEV
    per_block = TOK_DEV * TOPK
    slots = owners_count * CAP
    blocks = TOKENS // TOK_DEV
    favored = jax.random.randint(jax.random.fold_in(key, 1), (), 0, owners_count)

    def one_block(index):
        block_key = jax.random.fold_in(key, index + 2)
        key_slots, key_order, key_local = jax.random.split(block_key, 3)
        ranking = jax.random.permutation(key_slots, slots).astype(jnp.int32)
        slot_owner = jnp.arange(slots, dtype=jnp.int32) // CAP
        ranking = ranking + jnp.where(slot_owner == favored, slots, 0).astype(jnp.int32)
        chosen = lax.top_k(ranking, per_block)[1].astype(jnp.int32)
        owner_list = jax.random.permutation(key_order, chosen // CAP)
        local = jax.random.randint(key_local, (per_block,), 0, ROW_DEV)
        return (owner_list * ROW_DEV + local).astype(jnp.int32).reshape(TOK_DEV, TOPK)
    result = lax.map(one_block, jnp.arange(blocks, dtype=jnp.int32))
    return result.reshape(TOKENS, TOPK)


def block_scale(key, shape, pieces, low, high):
    def one(axis_at, parts):
        draws = jax.random.uniform(jax.random.fold_in(jax.random.fold_in(key, 6), axis_at), (parts,), jnp.float32, low / len(pieces), high / len(pieces))
        return jnp.repeat(jnp.exp(draws), shape[axis_at] // parts).reshape((-1,) + (1,) * (len(shape) - axis_at - 1))

    loudness = one(*pieces[0])
    for cut in pieces[1:]:
        loudness = loudness * one(*cut)
    return loudness


def gaussian(rng, extent, scale, bound, pieces=(), kind=jnp.bfloat16):
    array = scale * jax.random.normal(rng, extent, jnp.float32)
    if pieces:
        array = array * block_scale(rng, extent, pieces, -0.22, 0.18)
    return jnp.clip(array, -bound, bound).astype(kind)


def setup_inputs(seed: int = 0) -> dict:
    arg_keys = jax.random.split(jax.random.key(seed), 8)
    tokens = gaussian(arg_keys[0], (TOKENS, D), 1.0, 6.0, ((0, 64), (1, 4)))
    query_weight = gaussian(arg_keys[1], (D, KD), D ** -0.5, 0.125, ((0, 4),))
    keys_first = gaussian(arg_keys[2], (NA, H), H ** -0.5, 0.375)
    keys_second = gaussian(arg_keys[3], (NB, H), H ** -0.5, 0.375)
    values = gaussian(arg_keys[4], (ROWS, VD), 1.0, 6.0, ((0, 32), (1, 4)))
    picks = draw_picks(jax.random.fold_in(arg_keys[7], 71), 0)
    out_grad = gaussian(arg_keys[6], (TOKENS, VD), 1.0, 6.0, ((0, 64), (1, 4)))
    return {"tokens": tokens, "query_weight": query_weight, "keys_first": keys_first, "keys_second": keys_second, "values": values, "picks": picks, "out_grad": out_grad}


def reference(tokens, query_weight, keys_first, keys_second, values, picks, out_grad):
    query = jnp.dot(tokens, query_weight, preferred_element_type=jnp.float32).astype(jnp.bfloat16)
    query_a = query[:, :H]
    query_b = query[:, H:]
    first_scores = jnp.dot(query_a, keys_first.T, preferred_element_type=jnp.float32)
    second_scores = jnp.dot(query_b, keys_second.T, preferred_element_type=jnp.float32)
    first_index = (picks // NB).astype(jnp.int32)
    second_index = (picks % NB).astype(jnp.int32)
    score = jnp.take_along_axis(first_scores, first_index, 1) + jnp.take_along_axis(second_scores, second_index, 1)
    expo = jnp.exp(score)
    weight = expo / jnp.sum(expo, axis=1, keepdims=True)
    weight_b = weight.astype(jnp.bfloat16)
    block = math.gcd(TOKENS, 512)
    count = TOKENS // block

    def step(value_sum, inputs):
        pick_blk, weight_blk, grad_blk = inputs
        picked = jnp.take(values, pick_blk.reshape(-1), axis=0).reshape(block, TOPK, VD).astype(jnp.float32)
        mixed_blk = jnp.einsum("tk,tkv->tv", weight_blk.astype(jnp.float32), picked)
        grad_f = grad_blk.astype(jnp.float32)
        pick_grad = jnp.einsum("tv,tkv->tk", grad_f, picked)
        contrib = weight_blk.astype(jnp.float32)[:, :, None] * grad_f[:, None, :]
        value_sum = value_sum.at[pick_blk.reshape(-1)].add(contrib.reshape(block * TOPK, VD))
        return value_sum, (mixed_blk.astype(jnp.bfloat16), pick_grad)

    value_grad, (mixed, pick_grad) = lax.scan(
        step, jnp.zeros((ROWS, VD), jnp.float32),
        (picks.reshape(count, block, TOPK), weight_b.reshape(count, block, TOPK), out_grad.reshape(count, block, VD)))
    mixed = mixed.reshape(TOKENS, VD)
    pick_grad = pick_grad.reshape(TOKENS, TOPK)
    score_grad = weight * (pick_grad - jnp.sum(weight * pick_grad, axis=1, keepdims=True))
    row_ids = jnp.broadcast_to(jnp.arange(TOKENS, dtype=jnp.int32)[:, None], (TOKENS, TOPK))
    grad_a = jnp.zeros((TOKENS, NA), jnp.float32).at[row_ids, first_index].add(score_grad).astype(jnp.bfloat16)
    grad_b = jnp.zeros((TOKENS, NB), jnp.float32).at[row_ids, second_index].add(score_grad).astype(jnp.bfloat16)
    query_grad = jnp.concatenate([
        jnp.dot(grad_a, keys_first, preferred_element_type=jnp.float32),
        jnp.dot(grad_b, keys_second, preferred_element_type=jnp.float32)], axis=1).astype(jnp.bfloat16)
    token_grad = jnp.dot(query_grad, query_weight.T, preferred_element_type=jnp.float32).astype(jnp.bfloat16)
    query_weight_grad = jnp.dot(tokens.T, query_grad, preferred_element_type=jnp.float32)
    first_key_grad = jnp.dot(grad_a.T, query_a, preferred_element_type=jnp.float32)
    second_key_grad = jnp.dot(grad_b.T, query_b, preferred_element_type=jnp.float32)
    return (mixed, token_grad, query_weight_grad, first_key_grad, second_key_grad, value_grad)
```

```python
import functools

import jax
import jax.numpy as jnp
from jax import lax
from jax.experimental import pallas as pl
from jax.experimental.pallas import tpu as pltpu
from jax.sharding import PartitionSpec as P

BF = jnp.bfloat16
F32 = jnp.float32
I32 = jnp.int32
NT = (((1,), (1,)), ((), ()))
TN = (((0,), (0,)), ((), ()))
MIB = 1 << 20


def dot(x, y, dims=(((1,), (0,)), ((), ()))):
    return lax.dot_general(x, y, dims, preferred_element_type=F32)


def iota(shape, dim):
    return lax.broadcasted_iota(I32, shape, dim)


def whole(shape):
    return pl.BlockSpec(shape, lambda *_: (0,) * len(shape))


def route_kernel(
    row_dev, query_ref, first_ref, second_ref, picks_ref,
    lists_ref, rank_ref, weight_ref, score_b, score, lhs, slots,
):
    topk, tok = picks_ref.shape
    half = first_ref.shape[1]
    na, nb = first_ref.shape[0], second_ref.shape[0]
    n_row = lists_ref.shape[0]
    cap = slots.shape[0]
    query = query_ref[...]
    score_a = dot(first_ref[...], query[:, :half], NT)
    score_b[...] = dot(second_ref[...], query[:, half:], NT)

    def look_up(k, carry):
        pick = picks_ref[pl.ds(k, 1), :]
        in_a = iota((na, tok), 0) == pick // nb
        in_b = iota((nb, tok), 0) == pick % nb
        part_a = jnp.sum(jnp.where(in_a, score_a, 0.0), axis=0, keepdims=True)
        part_b = jnp.sum(jnp.where(in_b, score_b[...], 0.0), axis=0, keepdims=True)
        score[pl.ds(k, 1), :] = part_a + part_b
        return carry

    lax.fori_loop(0, topk, look_up, 0)
    expo = jnp.exp(score[...])
    weight = expo / jnp.sum(expo, axis=0, keepdims=True)
    weight_ref[...] = weight

    picks = picks_ref[...]
    owner = picks // row_dev
    local = picks % row_dev
    at_owner = iota((n_row, tok), 0)
    onehots = [(at_owner == owner[k : k + 1, :]) for k in range(topk)]
    stacked = jnp.concatenate([jnp.where(hot, 1.0, 0.0) for hot in onehots], axis=0).astype(BF)
    upto = jnp.where(iota((tok, tok), 0) <= iota((tok, tok), 1), 1.0, 0.0).astype(BF)
    running = dot(stacked, upto)
    totals = dot(stacked, jnp.ones((tok, tok), BF))
    base = jnp.full((n_row, tok), -1.0, F32)
    token = iota((n_row, tok), 1).astype(F32)
    for k in range(topk):
        hot = onehots[k]
        part = slice(k * n_row, (k + 1) * n_row)
        rank = jnp.sum(jnp.where(hot, running[part] + base, 0.0), axis=0, keepdims=True).astype(I32)
        base = base + totals[part]
        rank_ref[k : k + 1, :] = rank
        lanes = slice(k * tok, (k + 1) * tok)
        slots[:, lanes] = jnp.where(iota((cap, tok), 0) == rank, 1.0, 0.0).astype(BF)
        high = (local[k : k + 1, :] // 256).astype(F32)
        low = (local[k : k + 1, :] % 256).astype(F32)
        sent = [weight[k : k + 1, :], high, low, token]
        lhs[:, lanes] = jnp.concatenate([jnp.where(hot, v, 0.0) for v in sent], axis=0).astype(BF)
    listed = dot(lhs[...], slots[...], NT)
    weights = listed[:n_row]
    rows = listed[n_row : 2 * n_row] * 256.0 + listed[2 * n_row : 3 * n_row]
    tokens = listed[3 * n_row :]
    for at, part in enumerate((weights, rows, tokens)):
        lists_ref[:, 2 * at, :] = part[:, :128]
        lists_ref[:, 2 * at + 1, :] = part[:, 128:]
    lists_ref[:, 6, :] = jnp.zeros((n_row, 128), F32)
    lists_ref[:, 7, :] = jnp.zeros((n_row, 128), F32)


def route(query, keys_first, keys_second, picks_t, row_dev, n_row, cap):
    topk, tok = picks_t.shape
    return pl.pallas_call(
        functools.partial(route_kernel, row_dev),
        out_shape=(
            jax.ShapeDtypeStruct((n_row, 8, 128), F32),
            jax.ShapeDtypeStruct((topk, tok), I32),
            jax.ShapeDtypeStruct((topk, tok), F32),
        ),
        scratch_shapes=[
            pltpu.VMEM((keys_second.shape[0], tok), F32),
            pltpu.VMEM((topk, tok), F32),
            pltpu.VMEM((4 * n_row, topk * tok), BF),
            pltpu.VMEM((cap, topk * tok), BF),
        ],
        compiler_params=pltpu.CompilerParams(vmem_limit_bytes=32 * MIB),
        name="route",
    )(query, keys_first, keys_second, picks_t)


def listed(lists, at):
    return jnp.concatenate([lists[2 * at : 2 * at + 1, :], lists[2 * at + 1 : 2 * at + 2, :]], axis=1)


def owner_kernel(order_ref, lists_ref, grad_ref, values_ref, mixed_ref, pick_ref, spread_ref):
    cap = pick_ref.shape[2]
    rows = values_ref.shape[1]
    tok = grad_ref.shape[0]
    lists = lists_ref[0]
    weight = listed(lists, 0)
    row = listed(lists, 1).astype(I32)
    token = listed(lists, 2).astype(I32)
    hot = jnp.where(iota((rows, cap), 0) == row, 1.0, 0.0).astype(BF)
    picked = dot(values_ref[...], hot)
    at_token = iota((tok, cap), 0) == token
    spread = dot(grad_ref[...], jnp.where(at_token, 1.0, 0.0).astype(BF), TN)
    pick_ref[0] = jnp.sum(picked * spread, axis=0, keepdims=True)
    spread_ref[...] = spread.astype(BF)
    mixed_ref[...] = dot(
        jnp.where(at_token, weight, 0.0).astype(BF), picked.astype(BF), NT
    ).astype(BF)


def owner_side(order, lists, grads, values_t, cap):
    blocks = lists.shape[0]
    tok = grads.shape[0] // blocks
    cols, rows = values_t.shape
    return pl.pallas_call(
        owner_kernel,
        grid_spec=pltpu.PrefetchScalarGridSpec(
            num_scalar_prefetch=1,
            grid=(blocks,),
            in_specs=[
                pl.BlockSpec((1, 8, 128), lambda b, order: (order[b], 0, 0)),
                pl.BlockSpec((tok, cols), lambda b, order: (b, 0)),
                whole((cols, rows)),
            ],
            out_specs=[
                pl.BlockSpec((tok, cols), lambda b, order: (order[b], 0)),
                pl.BlockSpec((1, 1, cap), lambda b, order: (order[b], 0, 0)),
                pl.BlockSpec((cols, cap), lambda b, order: (0, order[b])),
            ],
        ),
        out_shape=(
            jax.ShapeDtypeStruct((blocks * tok, cols), BF),
            jax.ShapeDtypeStruct((blocks, 1, cap), F32),
            jax.ShapeDtypeStruct((cols, blocks * cap), BF),
        ),
        compiler_params=pltpu.CompilerParams(vmem_limit_bytes=32 * MIB),
        name="owner_side",
    )(order, lists, grads, values_t)


def scatter_kernel(lists_ref, spread_ref, out_ref):
    blocks = lists_ref.shape[0]
    tile = out_ref.shape[0]
    cap = spread_ref.shape[1] // blocks
    at_row = iota((tile, cap), 0) + pl.program_id(0) * tile
    total = jnp.zeros(out_ref.shape, F32)
    for b in range(blocks):
        lists = lists_ref[b]
        hot = jnp.where(at_row == listed(lists, 1).astype(I32), listed(lists, 0), 0.0).astype(BF)
        total = total + dot(hot, spread_ref[:, b * cap : (b + 1) * cap], NT)
    out_ref[...] = total


def scatter(lists, spread, rows, tile):
    cols, total = spread.shape
    return pl.pallas_call(
        scatter_kernel,
        grid=(rows // tile,),
        in_specs=[whole(lists.shape), whole(spread.shape)],
        out_specs=pl.BlockSpec((tile, cols), lambda r: (r, 0)),
        out_shape=jax.ShapeDtypeStruct((rows, cols), F32),
        compiler_params=pltpu.CompilerParams(vmem_limit_bytes=32 * MIB),
        name="scatter",
    )(lists, spread)


def grads_kernel(
    row_dev, parts_ref, rank_ref, picks_ref, weight_ref, query_ref, first_ref, second_ref,
    qw_ref, tokens_ref, token_grad_ref, qw_part_ref, first_part_ref, second_part_ref,
    slots, sums, grad_b,
):
    topk, tok = picks_ref.shape
    half = first_ref.shape[1]
    na, nb = first_ref.shape[0], second_ref.shape[0]
    cap = parts_ref.shape[2]
    n_row = parts_ref.shape[0]
    parts = parts_ref[...]
    by_slot = parts[:, 0, :]
    for m in range(1, parts_ref.shape[1]):
        by_slot = by_slot + parts[:, m, :]
    one = by_slot.astype(BF)
    rest = by_slot - one.astype(F32)
    two = rest.astype(BF)
    three = (rest - two.astype(F32)).astype(BF)
    for k in range(topk):
        slots[:, k * tok : (k + 1) * tok] = jnp.where(
            iota((cap, tok), 0) == rank_ref[k : k + 1, :], 1.0, 0.0
        ).astype(BF)
    sums[...] = dot(jnp.concatenate([one, two, three], axis=0), slots[...])
    picks = picks_ref[...]
    owner = picks // row_dev
    at_owner = iota((n_row, tok), 0)
    rows = []
    for k in range(topk):
        got = sums[:, k * tok : (k + 1) * tok]
        got = got[:n_row] + got[n_row : 2 * n_row] + got[2 * n_row :]
        rows.append(jnp.sum(jnp.where(at_owner == owner[k : k + 1, :], got, 0.0), axis=0, keepdims=True))
    pick_grad = jnp.concatenate(rows, axis=0)
    weight = weight_ref[...]
    score_grad = weight * (pick_grad - jnp.sum(weight * pick_grad, axis=0, keepdims=True))
    first_index = picks // nb
    second_index = picks % nb
    grad_a = jnp.zeros((na, tok), F32)
    for k in range(topk):
        grad_a = grad_a + jnp.where(
            iota((na, tok), 0) == first_index[k : k + 1, :], score_grad[k : k + 1, :], 0.0
        )
    grad_a = grad_a.astype(BF)
    tile = 128

    def one_tile(i, carry):
        at_b = iota((tile, tok), 0) + i * tile
        total = jnp.zeros((tile, tok), F32)
        for k in range(topk):
            total = total + jnp.where(
                at_b == second_index[k : k + 1, :], score_grad[k : k + 1, :], 0.0
            )
        grad_b[pl.ds(pl.multiple_of(i * tile, tile), tile), :] = total.astype(BF)
        return carry

    lax.fori_loop(0, nb // tile, one_tile, 0)
    query = query_ref[...]
    query_grad = jnp.concatenate(
        [dot(grad_a, first_ref[...], TN), dot(grad_b[...], second_ref[...], TN)], axis=1
    ).astype(BF)
    token_grad_ref[...] = dot(query_grad, qw_ref[...], NT).astype(BF)
    qw_part_ref[...] = dot(tokens_ref[...], query_grad, TN).astype(BF)
    first_part_ref[...] = dot(grad_a, query[:, :half]).astype(BF)
    second_part_ref[...] = dot(grad_b[...], query[:, half:]).astype(BF)


def grads(parts, rank, picks_t, weight, query, keys_first, keys_second, qw, tokens, row_dev):
    topk, tok = picks_t.shape
    cap = parts.shape[2]
    return pl.pallas_call(
        functools.partial(grads_kernel, row_dev),
        out_shape=(
            jax.ShapeDtypeStruct(tokens.shape, BF),
            jax.ShapeDtypeStruct(qw.shape, BF),
            jax.ShapeDtypeStruct(keys_first.shape, BF),
            jax.ShapeDtypeStruct(keys_second.shape, BF),
        ),
        scratch_shapes=[
            pltpu.VMEM((cap, topk * tok), BF),
            pltpu.VMEM((3 * parts.shape[0], topk * tok), F32),
            pltpu.VMEM((keys_second.shape[0], tok), BF),
        ],
        compiler_params=pltpu.CompilerParams(vmem_limit_bytes=32 * MIB),
        name="grads",
    )(parts, rank, picks_t, weight, query, keys_first, keys_second, qw, tokens)


def gather_blocks(block, n_x, n_z):
    def shift(sx, sz):
        return [
            (x * n_z + z, (x + sx) % n_x * n_z + (z + sz) % n_z)
            for x in range(n_x)
            for z in range(n_z)
        ]

    column = jnp.stack([block] + [lax.ppermute(block, "row", shift(s, 0)) for s in range(1, n_x)])
    held = {0: column}
    up = down = column
    for step in range(1, n_z // 2 + 1):
        up = lax.ppermute(up, "row", shift(0, 1))
        held[-step % n_z] = up
        if step < n_z // 2:
            down = lax.ppermute(down, "row", shift(0, -1))
            held[step] = down
    return held


def body(tokens, query_weight, keys_first, keys_second, values, picks, out_grad):
    tok, topk = picks.shape
    row_dev, cols = values.shape
    n_row, n_dim = lax.axis_size("row"), lax.axis_size("dim")
    cap = 2 * tok * topk // n_row
    n_x, n_z = 4, n_row // 4
    row_at = lax.axis_index("row")

    held = gather_blocks(out_grad, n_x, n_z)
    by_shift = jnp.stack([held[d] for d in range(n_z)])

    partial = dot(tokens, query_weight)
    pieces = lax.all_to_all(partial, "dim", 0, 0, tiled=True)
    quarter = jnp.sum(pieces.reshape(n_dim, tok // n_dim, -1), axis=0).astype(BF)
    query = lax.all_gather(quarter, "dim", tiled=True)
    picks_t = picks.T
    lists, rank, weight = route(query, keys_first, keys_second, picks_t, row_dev, n_row, cap)
    own_lists = lax.all_to_all(lists, "row", 0, 0, tiled=True)

    x_at, z_at = row_at // n_z, row_at % n_z
    order_d = jnp.arange(n_row, dtype=I32) // n_x
    order_s = jnp.arange(n_row, dtype=I32) % n_x
    order = (x_at - order_s) % n_x * n_z + (z_at + order_d) % n_z
    mixed_part, pick_part, spread = owner_side(
        order, own_lists, by_shift.reshape(n_row * tok, cols), values.T, cap
    )
    pick_sent = jnp.broadcast_to(pick_part, (n_row, n_dim, cap)).reshape(n_row * n_dim, cap)
    pick_parts = lax.all_to_all(pick_sent, ("row", "dim"), 0, 0, tiled=True).reshape(n_row, n_dim, cap)

    mixed_got = lax.all_to_all(mixed_part.reshape(n_row, tok, cols), "row", 0, 0, tiled=True)

    token_grad, qw_part, first_part, second_part = grads(
        pick_parts, rank, picks_t, weight, query, keys_first, keys_second, query_weight, tokens, row_dev
    )
    sums = jnp.concatenate([qw_part.reshape(-1, keys_first.shape[1]), first_part, second_part], axis=0)
    share = sums.shape[0] // n_row
    sums_got = lax.all_to_all(sums.reshape(n_row, share, -1), "row", 0, 0, tiled=True)
    summed = jnp.sum(sums_got.astype(F32), axis=0)
    summed = summed + lax.ppermute(summed, "dp", [(0, 1), (1, 0)])
    summed = jnp.broadcast_to(summed.astype(BF)[None], (n_row,) + summed.shape)
    sums_all = lax.all_to_all(summed, "row", 0, 0, tiled=True).reshape(sums.shape).astype(F32)
    n_qw = qw_part.size // keys_first.shape[1]
    qw_grad = sums_all[:n_qw].reshape(qw_part.shape)
    first_grad = sums_all[n_qw : n_qw + keys_first.shape[0]]
    second_grad = sums_all[n_qw + keys_first.shape[0] :]

    value_part = scatter(own_lists, spread, row_dev, 256)
    dp_at = lax.axis_index("dp")
    own = row_dev // 2
    theirs = lax.dynamic_slice_in_dim(value_part, (1 - dp_at) * own, own, 0)
    mine = lax.dynamic_slice_in_dim(value_part, dp_at * own, own, 0)
    value_grad = mine + lax.ppermute(theirs, "dp", [(0, 1), (1, 0)])
    mixed = jnp.sum(mixed_got.astype(F32), axis=0).astype(BF)
    return (mixed, token_grad, qw_grad, first_grad, second_grad, value_grad)


def solution(mesh):
    return jax.shard_map(
        body,
        mesh=mesh,
        in_specs=(
            P(("dp", "row"), "dim"),
            P("dim", None),
            P(),
            P(),
            P("row", "dim"),
            P(("dp", "row"), None),
            P(("dp", "row"), "dim"),
        ),
        out_specs=(
            P(("dp", "row"), "dim"),
            P(("dp", "row"), "dim"),
            P("dim", None),
            P(),
            P(),
            P(("row", "dp"), "dim"),
        ),
        check_vma=False,
    )
```

```python
import functools

import jax
import jax.numpy as jnp
from jax import lax
from jax.experimental import pallas as pl
from jax.experimental.pallas import tpu as pltpu
from jax.sharding import PartitionSpec as P

BF = jnp.bfloat16
F32 = jnp.float32
I32 = jnp.int32
NT = (((1,), (1,)), ((), ()))
TN = (((0,), (0,)), ((), ()))
MIB = 1 << 20


def dot(x, y, dims=(((1,), (0,)), ((), ()))):
    return lax.dot_general(x, y, dims, preferred_element_type=F32)


def iota(shape, dim):
    return lax.broadcasted_iota(I32, shape, dim)


def whole(shape):
    return pl.BlockSpec(shape, lambda *_: (0,) * len(shape))


def owner_order(picks, row_dev, n_z, n_x):
    owner = picks // row_dev
    return owner % n_z * n_x + owner // n_z


def small_iota(shape, dim):
    return iota(shape, dim).astype(F32).astype(BF)


def small(array):
    return array.astype(F32).astype(BF)


def hot_slots(slots, rank):
    topk, tok = rank.shape
    at_slot = small_iota((slots.shape[0], tok), 0)
    rank = small(rank)
    one, zero = jnp.ones((), BF), jnp.zeros((), BF)
    for at in range(topk):
        slots[:, at * tok : (at + 1) * tok] = jnp.where(at_slot == rank[at : at + 1, :], one, zero)


def place_kernel(row_dev, n_z, n_row, picks_ref, rank_ref):
    topk, tok = picks_ref.shape
    owner = owner_order(picks_ref[...], row_dev, n_z, n_row // n_z)
    at_owner = iota((n_row, tok), 0)
    onehots = [(at_owner == owner[k : k + 1, :]) for k in range(topk)]
    stacked = jnp.concatenate([jnp.where(hot, 1.0, 0.0) for hot in onehots], axis=0).astype(BF)
    upto = jnp.where(iota((tok, tok), 0) <= iota((tok, tok), 1), 1.0, 0.0).astype(BF)
    running = dot(stacked, upto)
    totals = dot(stacked, jnp.ones((tok, tok), BF))
    base = jnp.full((n_row, tok), -1.0, F32)
    for k in range(topk):
        part = slice(k * n_row, (k + 1) * n_row)
        rank = jnp.sum(jnp.where(onehots[k], running[part] + base, 0.0), axis=0, keepdims=True)
        base = base + totals[part]
        rank_ref[k : k + 1, :] = rank.astype(I32)


def place_picks(picks_t, row_dev, n_row, n_z):
    return pl.pallas_call(
        functools.partial(place_kernel, row_dev, n_z, n_row),
        out_shape=jax.ShapeDtypeStruct(picks_t.shape, I32),
        compiler_params=pltpu.CompilerParams(vmem_limit_bytes=12 * MIB),
        cost_estimate=pl.CostEstimate(flops=1_000_000_000, bytes_accessed=200_000, transcendentals=0),
        name="place_picks",
    )(picks_t)


def take_rows(table, index):
    topk, tok = index.shape
    within, group = index % 8, index // 8
    parts = [slice(q, q + 8) for q in range(0, topk, 8)]
    found = [jnp.zeros((8, tok), F32) for _ in parts]
    for g in range(table.shape[0] // 8):
        rows = table[8 * g : 8 * g + 8, :]
        for q, part in enumerate(parts):
            got = jnp.take_along_axis(rows, within[part], axis=0, mode="promise_in_bounds")
            found[q] = jnp.where(group[part] == g, got, found[q])
    return jnp.concatenate(found, axis=0)


def weigh_kernel(
    row_dev, n_x, query_ref, first_ref, second_ref, picks_ref, rank_ref, grad_ref,
    sent_ref, weight_ref, score_a, score_b, lhs, slots,
):
    topk, tok = picks_ref.shape
    half = first_ref.shape[1]
    nb = second_ref.shape[0]
    n_z = sent_ref.shape[0]
    query = query_ref[...]
    score_a[...] = dot(first_ref[...], query[:, :half], NT)
    score_b[...] = dot(second_ref[...], query[:, half:], NT)
    picks = picks_ref[...]
    score = take_rows(score_a, picks // nb) + take_rows(score_b, picks % nb)
    expo = jnp.exp(score)
    weight = expo / jnp.sum(expo, axis=0, keepdims=True)
    weight_ref[...] = weight
    weight = weight.astype(BF)
    local = picks % row_dev
    high, low = small(local // 256), small(local % 256)
    owner = small(owner_order(picks, row_dev, n_z, n_x))
    rows = (4 * n_z * n_x, tok)
    at_owner = small(iota(rows, 0) // 4)
    kind = small(iota(rows, 0) % 4)
    token = small_iota((1, tok), 1)
    zero = jnp.zeros((), BF)
    for k in range(topk):
        at = slice(k, k + 1)
        value = jnp.where(kind == 0.0, weight[at, :], jnp.where(
            kind == 1.0, high[at, :], jnp.where(kind == 2.0, low[at, :], token)))
        lhs[:, k * tok : (k + 1) * tok] = jnp.where(at_owner == owner[at, :], value, zero)
    hot_slots(slots, rank_ref[...])
    lists = dot(lhs[...], slots[...], NT).astype(BF)
    for z in range(n_z):
        sent_ref[z, :tok, :] = grad_ref[...]
        sent_ref[z, tok:, :] = lists[4 * n_x * z : 4 * n_x * (z + 1)]


def weigh(query, keys_first, keys_second, picks_t, rank, out_grad, row_dev, n_x, n_z, cap):
    topk, tok = picks_t.shape
    cols = out_grad.shape[1]
    return pl.pallas_call(
        functools.partial(weigh_kernel, row_dev, n_x),
        out_shape=(
            jax.ShapeDtypeStruct((n_z, tok + 4 * n_x, cols), BF),
            jax.ShapeDtypeStruct((topk, tok), F32),
        ),
        scratch_shapes=[
            pltpu.VMEM((keys_first.shape[0], tok), F32),
            pltpu.VMEM((keys_second.shape[0], tok), F32),
            pltpu.VMEM((4 * n_x * n_z, topk * tok), BF),
            pltpu.VMEM((cap, topk * tok), BF),
        ],
        compiler_params=pltpu.CompilerParams(vmem_limit_bytes=12 * MIB),
        cost_estimate=pl.CostEstimate(flops=4_000_000_000, bytes_accessed=1_000_000, transcendentals=4096),
        name="weigh",
    )(query, keys_first, keys_second, picks_t, rank, out_grad)


def listed(lists, x_own, kind):
    return lists[pl.ds(4 * x_own + kind, 1), :]


def owner_kernel(place_ref, got_ref, *rest):
    n_x = (len(rest) - 5) // 2
    value_refs = rest[: 2 * n_x]
    mixed_ref, pick_ref, values, hot, lists = rest[2 * n_x :]
    cap = pick_ref.shape[2]
    half = value_refs[0].shape[0]
    rows = value_refs[0].shape[1]
    tok = mixed_ref.shape[0]
    x_at, dp_at = place_ref[0], place_ref[1]

    @pl.when(pl.program_id(0) == 0)
    def _():
        for s in range(n_x):
            for at, ref in ((dp_at, value_refs[2 * s]), (1 - dp_at, value_refs[2 * s + 1])):
                values[s, pl.ds(pl.multiple_of(at * half, half), half), :] = ref[...]

    lists[...] = got_ref[0, tok:, :].astype(F32)
    count = small_iota((256, cap), 0)
    one, zero = jnp.ones((), BF), jnp.zeros((), BF)
    picked = []
    weights = []
    tokens = []
    for s in range(n_x):
        x_own = lax.rem(x_at - s + n_x, n_x)
        weights.append(listed(lists, x_own, 0))
        tokens.append(listed(lists, x_own, 3))
        high, low = listed(lists, x_own, 1), listed(lists, x_own, 2)
        for at in range(rows // 256):
            here = jnp.where(high == at, low, -1.0).astype(BF)
            hot[s, at * 256 : (at + 1) * 256, :] = jnp.where(count == here, one, zero)
        picked.append(dot(values[s], hot[s]))
    picked = jnp.concatenate(picked, axis=1)
    token = jnp.concatenate(tokens, axis=1).astype(BF)
    weight = jnp.concatenate(weights, axis=1).astype(BF)
    at_token = small_iota((tok, n_x * cap), 0) == token
    spread = dot(got_ref[0, :tok, :], jnp.where(at_token, one, zero), TN)
    pick = jnp.sum(picked * spread, axis=0, keepdims=True)
    for s in range(n_x):
        x_own = lax.rem(x_at - s + n_x, n_x)
        pick_ref[0, pl.ds(x_own, 1), :] = pick[:, s * cap : (s + 1) * cap]
    mixed_ref[...] = dot(jnp.where(at_token, weight, zero), picked.astype(BF), NT)


def owner_side(place, got, value_halves, cap):
    blocks, tall, cols = got.shape
    n_x = len(value_halves) // 2
    tok = tall - 4 * n_x
    half, rows = value_halves[0].shape
    return pl.pallas_call(
        owner_kernel,
        grid_spec=pltpu.PrefetchScalarGridSpec(
            num_scalar_prefetch=1,
            grid=(blocks,),
            in_specs=[pl.BlockSpec((1, tall, cols), lambda b, place: (b, 0, 0))]
            + [pl.BlockSpec((half, rows), lambda *_: (0, 0), pipeline_mode=pl.Buffered(1))] * (2 * n_x),
            out_specs=[
                pl.BlockSpec((tok, cols), lambda b, place: (b, 0)),
                pl.BlockSpec((1, n_x, cap), lambda b, place: (b, 0, 0)),
            ],
            scratch_shapes=[
                pltpu.VMEM((n_x, cols, rows), BF),
                pltpu.VMEM((n_x, rows, cap), BF),
                pltpu.VMEM((4 * n_x, cap), F32),
            ],
        ),
        out_shape=(
            jax.ShapeDtypeStruct((blocks * tok, cols), F32),
            jax.ShapeDtypeStruct((blocks, n_x, cap), F32),
        ),
        compiler_params=pltpu.CompilerParams(vmem_limit_bytes=20 * MIB),
        cost_estimate=pl.CostEstimate(flops=12_000_000_000, bytes_accessed=10_000_000, transcendentals=0),
        name="owner_side",
    )(place, got, *value_halves)


def scatter_kernel(n_x, place_ref, *rest):
    got_refs = rest[:n_x]
    out_ref, hot, spread, lists = rest[-4:]
    blocks, tall, cols = got_refs[0].shape
    kinds = lists.shape[1]
    cap = spread.shape[1] // (n_x * blocks)
    tok = tall - kinds
    x_own = place_ref[0]
    one, zero = jnp.ones((), BF), jnp.zeros((), BF)

    @pl.when(pl.program_id(0) == 0)
    def _():
        at_token = small_iota((tok, cap), 0)
        for s in range(n_x):
            for b in range(blocks):
                at = s * blocks + b
                lists[at] = got_refs[s][b, tok:, :].astype(F32)
                token = listed(lists.at[at], x_own, 3).astype(BF)
                spread[:, at * cap : (at + 1) * cap] = dot(
                    got_refs[s][b, :tok, :], jnp.where(at_token == token, one, zero), TN
                ).astype(BF)

    chunk = (place_ref[2] * pl.num_programs(0) + pl.program_id(0)).astype(F32)
    count = small_iota((256, cap), 0)
    for at in range(n_x * blocks):
        weight = listed(lists.at[at], x_own, 0).astype(BF)
        high, low = listed(lists.at[at], x_own, 1), listed(lists.at[at], x_own, 2)
        here = jnp.where(high == chunk, low, -1.0).astype(BF)
        hot[:, at * cap : (at + 1) * cap] = jnp.where(count == here, weight, zero)
    total = dot(hot[...], spread[...], NT)
    if len(rest) > n_x + 4:
        total = total + rest[n_x][...].astype(F32)
    out_ref[...] = total.astype(out_ref.dtype)


def scatter(place, gots, rows, kind, come=()):
    n_x = len(gots)
    blocks, tall, cols = gots[0].shape
    cap = cols
    tok = tall - 4 * n_x
    half = rows // 2
    each = pl.BlockSpec((256, cols), lambda r, place: (r, 0))
    fixed = pl.BlockSpec(gots[0].shape, lambda r, place: (0, 0, 0), pipeline_mode=pl.Buffered(1))
    return pl.pallas_call(
        functools.partial(scatter_kernel, n_x),
        grid_spec=pltpu.PrefetchScalarGridSpec(
            num_scalar_prefetch=1,
            grid=(half // 256,),
            in_specs=[fixed] * n_x + [each] * len(come),
            out_specs=each,
            scratch_shapes=[
                pltpu.VMEM((256, n_x * blocks * cap), BF),
                pltpu.VMEM((cols, n_x * blocks * cap), BF),
                pltpu.VMEM((n_x * blocks, 4 * n_x, cap), F32),
            ],
        ),
        out_shape=jax.ShapeDtypeStruct((half, cols), kind),
        compiler_params=pltpu.CompilerParams(vmem_limit_bytes=16 * MIB),
        cost_estimate=pl.CostEstimate(flops=5_000_000_000, bytes_accessed=6_000_000, transcendentals=0),
        name="scatter_mine" if come else "scatter_theirs",
    )(place, *gots, *come)


def grads_kernel(
    row_dev, n_z, parts_ref, rank_ref, picks_ref, weight_ref, query_ref, first_ref, second_ref,
    qw_ref, tokens_ref, token_grad_ref, part_ref, slots, sums, grad_b,
):
    topk, tok = picks_ref.shape
    half = first_ref.shape[1]
    na, nb = first_ref.shape[0], second_ref.shape[0]
    n_row, cap = parts_ref.shape[0] * parts_ref.shape[2], parts_ref.shape[3]
    by_slot = jnp.sum(parts_ref[...], axis=1).reshape(n_row, cap)
    one = by_slot.astype(BF)
    rest = by_slot - one.astype(F32)
    two = rest.astype(BF)
    three = (rest - two.astype(F32)).astype(BF)
    hot_slots(slots, rank_ref[...])
    sums[...] = dot(jnp.concatenate([one, two, three], axis=0), slots[...])
    picks = picks_ref[...]
    owner = owner_order(picks, row_dev, n_z, n_row // n_z)
    at_owner = iota((n_row, tok), 0)
    rows = []
    for k in range(topk):
        got = sums[:, k * tok : (k + 1) * tok]
        got = got[:n_row] + got[n_row : 2 * n_row] + got[2 * n_row :]
        rows.append(jnp.sum(jnp.where(at_owner == owner[k : k + 1, :], got, 0.0), axis=0, keepdims=True))
    pick_grad = jnp.concatenate(rows, axis=0)
    weight = weight_ref[...]
    score_grad = weight * (pick_grad - jnp.sum(weight * pick_grad, axis=0, keepdims=True))
    first_index = picks // nb
    second_index = picks % nb
    grad_a = jnp.zeros((na, tok), F32)
    for k in range(topk):
        grad_a = grad_a + jnp.where(
            iota((na, tok), 0) == first_index[k : k + 1, :], score_grad[k : k + 1, :], 0.0
        )
    grad_a = grad_a.astype(BF)
    tile = 128

    def one_tile(i, carry):
        at_b = iota((tile, tok), 0) + i * tile
        total = jnp.zeros((tile, tok), F32)
        for k in range(topk):
            total = total + jnp.where(
                at_b == second_index[k : k + 1, :], score_grad[k : k + 1, :], 0.0
            )
        grad_b[pl.ds(pl.multiple_of(i * tile, tile), tile), :] = total.astype(BF)
        return carry

    lax.fori_loop(0, nb // tile, one_tile, 0)
    query = query_ref[...]
    query_grad = jnp.concatenate(
        [dot(grad_a, first_ref[...], TN), dot(grad_b[...], second_ref[...], TN)], axis=1
    ).astype(BF)
    token_grad_ref[...] = dot(query_grad, qw_ref[...], NT).astype(BF)
    qw_part = dot(query_grad, tokens_ref[...], TN).astype(BF)
    first_part = dot(query[:, :half], grad_a, (((0,), (1,)), ((), ()))).astype(BF)
    second_part = dot(query[:, half:], grad_b[...], (((0,), (1,)), ((), ()))).astype(BF)
    n_qw = tokens_ref.shape[1]
    for h in range(2):
        part_ref[h, :, :n_qw] = qw_part[h * half : (h + 1) * half]
        part_ref[h, :, n_qw : n_qw + nb // 2] = second_part[:, h * (nb // 2) : (h + 1) * (nb // 2)]
        end = n_qw + (nb + na) // 2
        part_ref[h, :, n_qw + nb // 2 : end] = first_part[:, h * (na // 2) : (h + 1) * (na // 2)]
        part_ref[h, :, end:] = jnp.zeros((half, part_ref.shape[2] - end), BF)


def unfold_kernel(place_ref, mine_ref, other_ref, qw_ref, first_ref, second_ref):
    n_qw, n_second, n_first = qw_ref.shape[0], second_ref.shape[0] // 2, first_ref.shape[0] // 2
    half = mine_ref.shape[0]
    for side, ref in ((place_ref[1], mine_ref), (place_ref[2], other_ref)):
        qw_ref[:, pl.ds(pl.multiple_of(side * half, half), half)] = ref[:, :n_qw].astype(F32).T
        second_ref[pl.ds(pl.multiple_of(side * n_second, n_second), n_second), :] = (
            ref[:, n_qw : n_qw + n_second].astype(F32).T
        )
        first_ref[pl.ds(pl.multiple_of(side * n_first, n_first), n_first), :] = (
            ref[:, n_qw + n_second : n_qw + n_second + n_first].astype(F32).T
        )


def unfold(place, mine, other, shapes):
    return pl.pallas_call(
        unfold_kernel,
        in_specs=[pl.BlockSpec(memory_space=pltpu.SMEM)] + [pl.BlockSpec(memory_space=pltpu.VMEM)] * 2,
        out_shape=tuple(jax.ShapeDtypeStruct(shape, F32) for shape in shapes),
        compiler_params=pltpu.CompilerParams(vmem_limit_bytes=12 * MIB),
        name="unfold",
    )(place, mine, other)


def grads(parts, rank, picks_t, weight, query, keys_first, keys_second, qw, tokens, row_dev, n_z):
    topk, tok = picks_t.shape
    cap = parts.shape[3]
    n_row = parts.shape[0] * parts.shape[2]
    na, half = keys_first.shape
    nb = keys_second.shape[0]
    return pl.pallas_call(
        functools.partial(grads_kernel, row_dev, n_z),
        out_shape=(
            jax.ShapeDtypeStruct(tokens.shape, BF),
            jax.ShapeDtypeStruct((2, half, -(-(qw.shape[0] + (na + nb) // 2) // 128) * 128), BF),
        ),
        scratch_shapes=[
            pltpu.VMEM((cap, topk * tok), BF),
            pltpu.VMEM((3 * n_row, topk * tok), F32),
            pltpu.VMEM((nb, tok), BF),
        ],
        compiler_params=pltpu.CompilerParams(vmem_limit_bytes=16 * MIB),
        cost_estimate=pl.CostEstimate(flops=4_000_000_000, bytes_accessed=4_000_000, transcendentals=0),
        name="grads",
    )(parts, rank, picks_t, weight, query, keys_first, keys_second, qw, tokens)


def body(tokens, query_weight, keys_first, keys_second, values, picks, out_grad):
    tok, topk = picks.shape
    row_dev, cols = values.shape
    na, half = keys_first.shape
    nb = keys_second.shape[0]
    n_row, n_dim = lax.axis_size("row"), lax.axis_size("dim")
    cap = 2 * tok * topk // n_row
    n_x = 4
    n_z = n_row // n_x
    row_at, dp_at = lax.axis_index("row"), lax.axis_index("dp")
    place = jnp.stack([row_at // n_z, dp_at, 1 - dp_at, row_at % n_z]).astype(I32)
    rings = [[x * n_z + z for z in range(n_z)] for x in range(n_x)]
    planes = [[r * n_dim + m for r in ring for m in range(n_dim)] for ring in rings]

    def other_core(array):
        return lax.ppermute(array, "dp", [(0, 1), (1, 0)])

    def along_x(array, shift):
        pairs = [(x * n_z + z, (x + shift) % n_x * n_z + z) for x in range(n_x) for z in range(n_z)]
        return lax.ppermute(array, "row", pairs)

    def along_dim(array, shift):
        return lax.ppermute(array, "dim", [(m, (m + shift) % n_dim) for m in range(n_dim)])

    partial = dot(tokens, query_weight)
    partial, values = lax.optimization_barrier((partial, values))
    near = [along_dim(partial, s) for s in (1, 2, 3)]
    picks_t = picks.T
    rank = place_picks(picks_t, row_dev, n_row, n_z)

    values_t = values.T
    own_half = lax.dynamic_slice_in_dim(values_t, dp_at * (cols // 2), cols // 2, 0)
    other_half = lax.dynamic_slice_in_dim(values_t, (1 - dp_at) * (cols // 2), cols // 2, 0)
    value_halves = [own_half, other_half]
    for s in range(1, n_x):
        got = along_x(own_half, s)
        value_halves += [got, other_core(got)]

    query = ((partial + near[1]) + (near[0] + near[2])).astype(BF)
    query, rank = lax.optimization_barrier((query, rank))
    sent, weight = weigh(
        query, keys_first, keys_second, picks_t, rank, out_grad, row_dev, n_x, n_z, cap
    )
    got = lax.all_to_all(sent, "row", 0, 0, tiled=True, axis_index_groups=rings)

    mixed_part, pick_part = owner_side(place, got, value_halves, cap)
    gots = [got] + [along_x(got, s) for s in range(1, n_x)]
    pick_sent = jnp.broadcast_to(pick_part[:, None], (n_z, n_dim, n_x, cap))
    pick_parts = lax.all_to_all(
        pick_sent.reshape(n_z * n_dim, n_x, cap), ("row", "dim"), 0, 0, tiled=True,
        axis_index_groups=planes,
    ).reshape(n_z, n_dim, n_x, cap)

    mixed = lax.psum_scatter(
        mixed_part, "row", tiled=True, axis_index_groups=rings
    ).astype(BF)
    pick_parts, gots = lax.optimization_barrier((pick_parts, gots))
    token_grad, sums = grads(
        pick_parts, rank, picks_t, weight, query, keys_first, keys_second, query_weight, tokens,
        row_dev, n_z,
    )
    theirs = lax.dynamic_index_in_dim(sums, 1 - dp_at, 0, keepdims=False)
    mine = lax.dynamic_index_in_dim(sums, dp_at, 0, keepdims=False)
    mine = (mine.astype(F32) + other_core(theirs).astype(F32)).astype(BF)
    shape = (n_row, half // n_row, mine.shape[1])
    received = lax.all_to_all(mine.reshape(shape), "row", 0, 0, tiled=True)
    summed = jnp.sum(received.astype(F32), axis=0).astype(BF)
    come = other_core(scatter(place, gots, row_dev, BF))
    summed, come = lax.optimization_barrier((summed, come))
    summed = jnp.broadcast_to(summed[None], shape)
    mine = lax.all_to_all(summed, "row", 0, 0, tiled=True).reshape(mine.shape)
    own_place = jnp.stack([row_at // n_z, dp_at, dp_at]).astype(I32)
    value_grad = scatter(own_place, gots, row_dev, F32, (come,))
    mine, mixed, value_grad = lax.optimization_barrier((mine, mixed, value_grad))
    other = other_core(mine)
    qw_grad, first_grad, second_grad = unfold(
        place, mine, other, (query_weight.shape, keys_first.shape, keys_second.shape)
    )
    return (mixed, token_grad, qw_grad, first_grad, second_grad, value_grad)


def solution(mesh):
    return jax.shard_map(
        body,
        mesh=mesh,
        in_specs=(
            P(("dp", "row"), "dim"),
            P("dim", None),
            P(),
            P(),
            P("row", "dim"),
            P(("dp", "row"), None),
            P(("dp", "row"), "dim"),
        ),
        out_specs=(
            P(("dp", "row"), "dim"),
            P(("dp", "row"), "dim"),
            P("dim", None),
            P(),
            P(),
            P(("row", "dp"), "dim"),
        ),
        check_vma=False,
    )
```

```python
import functools

import jax
import jax.numpy as jnp
from jax import lax
from jax.experimental import pallas as pl
from jax.experimental.pallas import tpu as pltpu
from jax.sharding import PartitionSpec as P

BF = jnp.bfloat16
F32 = jnp.float32
I32 = jnp.int32
NT = (((1,), (1,)), ((), ()))
TN = (((0,), (0,)), ((), ()))
MIB = 1 << 20


def dot(x, y, dims=(((1,), (0,)), ((), ()))):
    return lax.dot_general(x, y, dims, preferred_element_type=F32)


def iota(shape, dim):
    return lax.broadcasted_iota(I32, shape, dim)


def whole(shape):
    return pl.BlockSpec(shape, lambda *_: (0,) * len(shape))


def owner_order(picks, row_dev, n_z, n_x):
    owner = picks // row_dev
    return owner % n_z * n_x + owner // n_z


def small_iota(shape, dim):
    return iota(shape, dim).astype(F32).astype(BF)


def small(array):
    return array.astype(F32).astype(BF)


def hot_slots(slots, rank):
    topk, tok = rank.shape
    at_slot = small_iota((slots.shape[0], tok), 0)
    rank = small(rank)
    one, zero = jnp.ones((), BF), jnp.zeros((), BF)
    for at in range(topk):
        slots[:, at * tok : (at + 1) * tok] = jnp.where(at_slot == rank[at : at + 1, :], one, zero)


def place_kernel(row_dev, n_z, n_row, picks_ref, rank_ref):
    topk, tok = picks_ref.shape
    owner = owner_order(picks_ref[...], row_dev, n_z, n_row // n_z)
    at_owner = iota((n_row, tok), 0)
    onehots = [(at_owner == owner[k : k + 1, :]) for k in range(topk)]
    stacked = jnp.concatenate([jnp.where(hot, 1.0, 0.0) for hot in onehots], axis=0).astype(BF)
    upto = jnp.where(iota((tok, tok), 0) <= iota((tok, tok), 1), 1.0, 0.0).astype(BF)
    running = dot(stacked, upto)
    totals = dot(stacked, jnp.ones((tok, tok), BF))
    base = jnp.full((n_row, tok), -1.0, F32)
    for k in range(topk):
        part = slice(k * n_row, (k + 1) * n_row)
        rank = jnp.sum(jnp.where(onehots[k], running[part] + base, 0.0), axis=0, keepdims=True)
        base = base + totals[part]
        rank_ref[k : k + 1, :] = rank.astype(I32)


def place_picks(picks_t, row_dev, n_row, n_z):
    return pl.pallas_call(
        functools.partial(place_kernel, row_dev, n_z, n_row),
        out_shape=jax.ShapeDtypeStruct(picks_t.shape, I32),
        compiler_params=pltpu.CompilerParams(vmem_limit_bytes=12 * MIB),
        cost_estimate=pl.CostEstimate(flops=1_000_000_000, bytes_accessed=200_000, transcendentals=0),
        name="place_picks",
    )(picks_t)


def take_rows(table, index):
    topk, tok = index.shape
    within, group = index % 8, index // 8
    parts = [slice(q, q + 8) for q in range(0, topk, 8)]
    found = [jnp.zeros((8, tok), F32) for _ in parts]
    for g in range(table.shape[0] // 8):
        rows = table[8 * g : 8 * g + 8, :]
        for q, part in enumerate(parts):
            got = jnp.take_along_axis(rows, within[part], axis=0, mode="promise_in_bounds")
            found[q] = jnp.where(group[part] == g, got, found[q])
    return jnp.concatenate(found, axis=0)


def weigh_kernel(
    row_dev, n_x, query_ref, first_ref, second_ref, picks_ref, rank_ref, grad_ref,
    sent_ref, weight_ref, score_a, score_b, lhs, slots,
):
    topk, tok = picks_ref.shape
    half = first_ref.shape[1]
    nb = second_ref.shape[0]
    n_z = sent_ref.shape[0]
    query = query_ref[...]
    score_a[...] = dot(first_ref[...], query[:, :half], NT)
    score_b[...] = dot(second_ref[...], query[:, half:], NT)
    picks = picks_ref[...]
    score = take_rows(score_a, picks // nb) + take_rows(score_b, picks % nb)
    expo = jnp.exp(score)
    weight = expo / jnp.sum(expo, axis=0, keepdims=True)
    weight_ref[...] = weight
    weight = weight.astype(BF)
    local = picks % row_dev
    high, low = small(local // 256), small(local % 256)
    owner = small(owner_order(picks, row_dev, n_z, n_x))
    rows = (4 * n_z * n_x, tok)
    at_owner = small(iota(rows, 0) // 4)
    kind = small(iota(rows, 0) % 4)
    token = small_iota((1, tok), 1)
    zero = jnp.zeros((), BF)
    for k in range(topk):
        at = slice(k, k + 1)
        value = jnp.where(kind == 0.0, weight[at, :], jnp.where(
            kind == 1.0, high[at, :], jnp.where(kind == 2.0, low[at, :], token)))
        lhs[:, k * tok : (k + 1) * tok] = jnp.where(at_owner == owner[at, :], value, zero)
    hot_slots(slots, rank_ref[...])
    lists = dot(lhs[...], slots[...], NT).astype(BF)
    for z in range(n_z):
        sent_ref[z, :tok, :] = grad_ref[...]
        sent_ref[z, tok:, :] = lists[4 * n_x * z : 4 * n_x * (z + 1)]


def weigh(query, keys_first, keys_second, picks_t, rank, out_grad, row_dev, n_x, n_z, cap):
    topk, tok = picks_t.shape
    cols = out_grad.shape[1]
    return pl.pallas_call(
        functools.partial(weigh_kernel, row_dev, n_x),
        out_shape=(
            jax.ShapeDtypeStruct((n_z, tok + 4 * n_x, cols), BF),
            jax.ShapeDtypeStruct((topk, tok), F32),
        ),
        scratch_shapes=[
            pltpu.VMEM((keys_first.shape[0], tok), F32),
            pltpu.VMEM((keys_second.shape[0], tok), F32),
            pltpu.VMEM((4 * n_x * n_z, topk * tok), BF),
            pltpu.VMEM((cap, topk * tok), BF),
        ],
        compiler_params=pltpu.CompilerParams(vmem_limit_bytes=12 * MIB),
        cost_estimate=pl.CostEstimate(flops=4_000_000_000, bytes_accessed=1_000_000, transcendentals=4096),
        name="weigh",
    )(query, keys_first, keys_second, picks_t, rank, out_grad)


def listed(lists, x_own, kind):
    return lists[pl.ds(4 * x_own + kind, 1), :]


def owner_kernel(place_ref, got_ref, *rest):
    n_x = (len(rest) - 6) // 2
    value_refs = rest[: 2 * n_x]
    mixed_ref, pick_ref, values, hot, lists, done = rest[2 * n_x :]
    cap = 2 * pick_ref.shape[2]
    half = value_refs[0].shape[0]
    rows = value_refs[0].shape[1]
    tok = mixed_ref.shape[0]
    x_at, dp_at = place_ref[0], place_ref[1]

    @pl.when(pl.program_id(0) == 0)
    def _():
        copies = []
        for i, ref in enumerate(value_refs):
            at = pl.multiple_of((dp_at if i % 2 == 0 else 1 - dp_at) * half, half)
            place = values.at[i // 2, pl.ds(at, half), :]
            copies.append(pltpu.make_async_copy(ref, place, done.at[i]))
        for copy in copies:
            copy.start()
        for copy in copies:
            copy.wait()

    lists[...] = got_ref[0, tok:, :].astype(F32)
    count = small_iota((256, cap), 0)
    one, zero = jnp.ones((), BF), jnp.zeros((), BF)
    picked = []
    weights = []
    tokens = []
    for s in range(n_x):
        x_own = lax.rem(x_at - s + n_x, n_x)
        weights.append(listed(lists, x_own, 0))
        tokens.append(listed(lists, x_own, 3))
        high, low = listed(lists, x_own, 1), listed(lists, x_own, 2)
        for at in range(rows // 256):
            here = jnp.where(high == at, low, -1.0).astype(BF)
            hot[s, at * 256 : (at + 1) * 256, :] = jnp.where(count == here, one, zero)
        picked.append(dot(values[s], hot[s]))
    picked = jnp.concatenate(picked, axis=1)
    token = jnp.concatenate(tokens, axis=1).astype(BF)
    weight = jnp.concatenate(weights, axis=1).astype(BF)
    at_token = small_iota((tok, n_x * cap), 0) == token
    spread = dot(got_ref[0, :tok, :], jnp.where(at_token, one, zero), TN)
    pick = jnp.sum(picked * spread, axis=0, keepdims=True)
    for s in range(n_x):
        x_own = lax.rem(x_at - s + n_x, n_x)
        for half_at in range(2):
            at = s * cap + half_at * 128
            pick_ref[0, pl.ds(2 * x_own + half_at, 1), :] = pick[:, at : at + 128]
    mixed_ref[...] = dot(jnp.where(at_token, weight, zero), picked.astype(BF), NT)


def owner_side(place, got, value_halves, cap):
    blocks, tall, cols = got.shape
    n_x = len(value_halves) // 2
    tok = tall - 4 * n_x
    half, rows = value_halves[0].shape
    return pl.pallas_call(
        owner_kernel,
        grid_spec=pltpu.PrefetchScalarGridSpec(
            num_scalar_prefetch=1,
            grid=(blocks,),
            in_specs=[pl.BlockSpec((1, tall, cols), lambda b, place: (b, 0, 0))]
            + [pl.BlockSpec(memory_space=pltpu.HBM)] * (2 * n_x),
            out_specs=[
                pl.BlockSpec((tok, cols), lambda b, place: (b, 0)),
                pl.BlockSpec((1, 2 * n_x, cap // 2), lambda b, place: (b, 0, 0)),
            ],
            scratch_shapes=[
                pltpu.VMEM((n_x, cols, rows), BF),
                pltpu.VMEM((n_x, rows, cap), BF),
                pltpu.VMEM((4 * n_x, cap), F32),
                pltpu.SemaphoreType.DMA((2 * n_x,)),
            ],
        ),
        out_shape=(
            jax.ShapeDtypeStruct((blocks * tok, cols), F32),
            jax.ShapeDtypeStruct((blocks, 2 * n_x, cap // 2), F32),
        ),
        compiler_params=pltpu.CompilerParams(vmem_limit_bytes=20 * MIB),
        cost_estimate=pl.CostEstimate(flops=12_000_000_000, bytes_accessed=10_000_000, transcendentals=0),
        name="owner_side",
    )(place, got, *value_halves)


def scatter_kernel(n_after, place_ref, got_ref, *rest):
    come_refs, (out_ref, hot, spread, lists) = rest[n_after:-4], rest[-4:]
    blocks, kinds, cap = lists.shape
    tok = got_ref.shape[1] - kinds
    x_own = place_ref[0]
    one, zero = jnp.ones((), BF), jnp.zeros((), BF)

    @pl.when(pl.program_id(0) == 0)
    def _():
        at_token = small_iota((tok, cap), 0)
        for at in range(blocks):
            lists[at] = got_ref[at, tok:, :].astype(F32)
            token = listed(lists.at[at], x_own, 3).astype(BF)
            spread[:, at * cap : (at + 1) * cap] = dot(
                got_ref[at, :tok, :], jnp.where(at_token == token, one, zero), TN
            ).astype(BF)

    chunk = (place_ref[2] * pl.num_programs(0) + pl.program_id(0)).astype(F32)
    count = small_iota((256, cap), 0)
    for at in range(blocks):
        weight = listed(lists.at[at], x_own, 0).astype(BF)
        high, low = listed(lists.at[at], x_own, 1), listed(lists.at[at], x_own, 2)
        here = jnp.where(high == chunk, low, -1.0).astype(BF)
        hot[:, at * cap : (at + 1) * cap] = jnp.where(count == here, weight, zero)
    total = dot(hot[...], spread[...], NT)
    for come_ref in come_refs:
        total = total + come_ref[...]
    out_ref[...] = total.astype(out_ref.dtype)


def scatter(place, got, after, rows, n_x, come=()):
    blocks, tall, cols = got.shape
    cap = cols
    half = rows // 2
    each = pl.BlockSpec((256, cols), lambda r, place: (r, 0))
    fixed = pl.BlockSpec(got.shape, lambda r, place: (0, 0, 0), pipeline_mode=pl.Buffered(1))
    return pl.pallas_call(
        functools.partial(scatter_kernel, len(after)),
        grid_spec=pltpu.PrefetchScalarGridSpec(
            num_scalar_prefetch=1,
            grid=(half // 256,),
            in_specs=[fixed] + [pl.BlockSpec(memory_space=pl.ANY)] * len(after) + [each] * len(come),
            out_specs=each,
            scratch_shapes=[
                pltpu.VMEM((256, blocks * cap), BF),
                pltpu.VMEM((cols, blocks * cap), BF),
                pltpu.VMEM((blocks, 4 * n_x, cap), F32),
            ],
        ),
        out_shape=jax.ShapeDtypeStruct((half, cols), F32),
        compiler_params=pltpu.CompilerParams(vmem_limit_bytes=16 * MIB),
        cost_estimate=pl.CostEstimate(flops=5_000_000_000, bytes_accessed=6_000_000, transcendentals=0),
        name="scatter_mine" if come else "scatter_theirs",
    )(place, got, *after, *come)


def grads_kernel(
    row_dev, n_z, place_ref, parts_ref, rank_ref, picks_ref, weight_ref, query_ref, first_ref, second_ref,
    qw_ref, tokens_ref, token_grad_ref, mine_ref, theirs_ref, slots, sums, grad_b, halves,
):
    topk, tok = picks_ref.shape
    half = first_ref.shape[1]
    na, nb = first_ref.shape[0], second_ref.shape[0]
    n_row, cap = parts_ref.shape[0] * parts_ref.shape[2] // 2, 2 * parts_ref.shape[3]
    halves[...] = jnp.sum(parts_ref[...], axis=1).reshape(2 * n_row, cap // 2)
    by_slot = jnp.concatenate(
        [halves[pl.ds(0, n_row, stride=2), :], halves[pl.ds(1, n_row, stride=2), :]], axis=1
    )
    one = by_slot.astype(BF)
    rest = by_slot - one.astype(F32)
    two = rest.astype(BF)
    three = (rest - two.astype(F32)).astype(BF)
    hot_slots(slots, rank_ref[...])
    sums[...] = dot(jnp.concatenate([one, two, three], axis=0), slots[...])
    picks = picks_ref[...]
    owner = owner_order(picks, row_dev, n_z, n_row // n_z)
    at_owner = iota((n_row, tok), 0)
    rows = []
    for k in range(topk):
        got = sums[:, k * tok : (k + 1) * tok]
        got = got[:n_row] + got[n_row : 2 * n_row] + got[2 * n_row :]
        rows.append(jnp.sum(jnp.where(at_owner == owner[k : k + 1, :], got, 0.0), axis=0, keepdims=True))
    pick_grad = jnp.concatenate(rows, axis=0)
    weight = weight_ref[...]
    score_grad = weight * (pick_grad - jnp.sum(weight * pick_grad, axis=0, keepdims=True))
    first_index = picks // nb
    second_index = picks % nb
    grad_a = jnp.zeros((na, tok), F32)
    for k in range(topk):
        grad_a = grad_a + jnp.where(
            iota((na, tok), 0) == first_index[k : k + 1, :], score_grad[k : k + 1, :], 0.0
        )
    grad_a = grad_a.astype(BF)
    tile = 128

    def one_tile(i, carry):
        at_b = iota((tile, tok), 0) + i * tile
        total = jnp.zeros((tile, tok), F32)
        for k in range(topk):
            total = total + jnp.where(
                at_b == second_index[k : k + 1, :], score_grad[k : k + 1, :], 0.0
            )
        grad_b[pl.ds(pl.multiple_of(i * tile, tile), tile), :] = total.astype(BF)
        return carry

    lax.fori_loop(0, nb // tile, one_tile, 0)
    query = query_ref[...]
    query_grad = jnp.concatenate(
        [dot(grad_a, first_ref[...], TN), dot(grad_b[...], second_ref[...], TN)], axis=1
    ).astype(BF)
    token_grad_ref[...] = dot(query_grad, qw_ref[...], NT).astype(BF)
    n_qw = tokens_ref.shape[1]
    at_second, end = n_qw + nb // 2, n_qw + (nb + na) // 2
    query_a, query_b = query[:, :half], query[:, half:]
    parts = []
    for h in range(2):
        qw_part = dot(query_grad[:, h * half : (h + 1) * half], tokens_ref[...], TN)
        own_b = slice(h * (nb // 2), (h + 1) * (nb // 2))
        second_part = dot(query_b, grad_b[own_b, :], (((0,), (1,)), ((), ())))
        first_part = dot(query_a, grad_a[h * (na // 2) : (h + 1) * (na // 2)], (((0,), (1,)), ((), ())))
        rest = jnp.zeros((half, mine_ref.shape[1] - end), F32)
        parts.append(jnp.concatenate([qw_part, second_part, first_part, rest], axis=1))
    swap = place_ref[1] == 1
    mine_ref[...] = jnp.where(swap, parts[1], parts[0])
    theirs_ref[...] = jnp.where(swap, parts[0], parts[1]).astype(theirs_ref.dtype)


def grads(place, parts, rank, picks_t, weight, query, keys_first, keys_second, qw, tokens, row_dev, n_z):
    topk, tok = picks_t.shape
    cap = 2 * parts.shape[3]
    n_row = parts.shape[0] * parts.shape[2] // 2
    na, half = keys_first.shape
    nb = keys_second.shape[0]
    folded = (half, -(-(qw.shape[0] + (na + nb) // 2) // 128) * 128)
    return pl.pallas_call(
        functools.partial(grads_kernel, row_dev, n_z),
        in_specs=[pl.BlockSpec(memory_space=pltpu.SMEM)] + [pl.BlockSpec(memory_space=pltpu.VMEM)] * 9,
        out_shape=(
            jax.ShapeDtypeStruct(tokens.shape, BF),
            jax.ShapeDtypeStruct(folded, F32),
            jax.ShapeDtypeStruct(folded, BF),
        ),
        scratch_shapes=[
            pltpu.VMEM((cap, topk * tok), BF),
            pltpu.VMEM((3 * n_row, topk * tok), F32),
            pltpu.VMEM((nb, tok), BF),
            pltpu.VMEM((2 * n_row, cap // 2), F32),
        ],
        compiler_params=pltpu.CompilerParams(vmem_limit_bytes=16 * MIB),
        cost_estimate=pl.CostEstimate(flops=4_000_000_000, bytes_accessed=4_000_000, transcendentals=0),
        name="grads",
    )(place, parts, rank, picks_t, weight, query, keys_first, keys_second, qw, tokens)


def unfold_kernel(place_ref, mine_ref, other_ref, qw_ref, first_ref, second_ref):
    n_qw, n_second, n_first = qw_ref.shape[0], second_ref.shape[0] // 2, first_ref.shape[0] // 2
    half = mine_ref.shape[0]
    for side, ref in ((place_ref[1], mine_ref), (place_ref[2], other_ref)):
        qw_ref[:, pl.ds(pl.multiple_of(side * half, half), half)] = ref[:, :n_qw].astype(F32).T
        second_ref[pl.ds(pl.multiple_of(side * n_second, n_second), n_second), :] = (
            ref[:, n_qw : n_qw + n_second].astype(F32).T
        )
        first_ref[pl.ds(pl.multiple_of(side * n_first, n_first), n_first), :] = (
            ref[:, n_qw + n_second : n_qw + n_second + n_first].astype(F32).T
        )


def unfold(place, mine, other, shapes):
    return pl.pallas_call(
        unfold_kernel,
        in_specs=[pl.BlockSpec(memory_space=pltpu.SMEM)] + [pl.BlockSpec(memory_space=pltpu.VMEM)] * 2,
        out_shape=tuple(jax.ShapeDtypeStruct(shape, F32) for shape in shapes),
        compiler_params=pltpu.CompilerParams(vmem_limit_bytes=12 * MIB),
        name="unfold",
    )(place, mine, other)


def body(tokens, query_weight, keys_first, keys_second, values, picks, out_grad):
    tok, topk = picks.shape
    row_dev, cols = values.shape
    na, half = keys_first.shape
    nb = keys_second.shape[0]
    n_row, n_dim = lax.axis_size("row"), lax.axis_size("dim")
    cap = 2 * tok * topk // n_row
    n_x = 4
    n_z = n_row // n_x
    row_at, dp_at = lax.axis_index("row"), lax.axis_index("dp")
    place = jnp.stack([row_at // n_z, dp_at, 1 - dp_at, row_at % n_z]).astype(I32)
    rings = [[x * n_z + z for z in range(n_z)] for x in range(n_x)]
    columns = [[x * n_z + z for x in range(n_x)] for z in range(n_z)]
    planes = [[r * n_dim + m for r in ring for m in range(n_dim)] for ring in rings]

    def other_core(array):
        return lax.ppermute(array, "dp", [(0, 1), (1, 0)])

    def along_x(array, shift):
        pairs = [(x * n_z + z, (x + shift) % n_x * n_z + z) for x in range(n_x) for z in range(n_z)]
        return lax.ppermute(array, "row", pairs)

    def along_dim(array, shift):
        return lax.ppermute(array, "dim", [(m, (m + shift) % n_dim) for m in range(n_dim)])

    partial = dot(tokens, query_weight)
    partial, values = lax.optimization_barrier((partial, values))
    near = [along_dim(partial, s) for s in (1, 2, 3)]
    picks_t = picks.T
    rank = place_picks(picks_t, row_dev, n_row, n_z)

    values_t = values.T
    own_half = lax.dynamic_slice_in_dim(values_t, dp_at * (cols // 2), cols // 2, 0)
    other_half = lax.dynamic_slice_in_dim(values_t, (1 - dp_at) * (cols // 2), cols // 2, 0)
    value_halves = [own_half, other_half]
    for s in range(1, n_x):
        got = along_x(own_half, s)
        value_halves += [got, other_core(got)]

    query = ((partial + near[1]) + (near[0] + near[2])).astype(BF)
    query, rank = lax.optimization_barrier((query, rank))
    sent, weight = weigh(
        query, keys_first, keys_second, picks_t, rank, out_grad, row_dev, n_x, n_z, cap
    )
    got = lax.all_to_all(sent, "row", 0, 0, tiled=True, axis_index_groups=rings)

    corners = [part[:8, :128] for part in value_halves[3::2]]
    late, corners = lax.optimization_barrier((got, corners))
    got_x = lax.all_gather(late, "row", tiled=True, axis_index_groups=columns)
    mixed_part, pick_part = owner_side(place, got, value_halves, cap)
    pick_sent = jnp.broadcast_to(pick_part[:, None], (n_z, n_dim) + pick_part.shape[1:])
    pick_parts = lax.all_to_all(
        pick_sent.reshape((n_z * n_dim,) + pick_part.shape[1:]), ("row", "dim"), 0, 0, tiled=True,
        axis_index_groups=planes,
    ).reshape(pick_sent.shape)

    mixed = lax.psum_scatter(
        mixed_part, "row", tiled=True, axis_index_groups=rings
    ).astype(BF)
    token_grad, mine, theirs = grads(
        place, pick_parts, rank, picks_t, weight, query, keys_first, keys_second, query_weight, tokens,
        row_dev, n_z,
    )
    mine = (mine + other_core(theirs).astype(F32)).astype(BF)
    shape = (n_row, half // n_row, mine.shape[1])
    received = lax.all_to_all(mine.reshape(shape), "row", 0, 0, tiled=True)
    summed = jnp.sum(received.astype(F32), axis=0).astype(BF)
    come = other_core(scatter(place, got_x, corners, row_dev, n_x))
    summed, come = lax.optimization_barrier((summed, come))
    summed = jnp.broadcast_to(summed[None], shape)
    mine = lax.all_to_all(summed, "row", 0, 0, tiled=True).reshape(mine.shape)
    own_place = jnp.stack([row_at // n_z, dp_at, dp_at]).astype(I32)
    value_grad = scatter(own_place, got_x, corners, row_dev, n_x, (come,))
    mine, mixed, value_grad = lax.optimization_barrier((mine, mixed, value_grad))
    other = other_core(mine)
    qw_grad, first_grad, second_grad = unfold(
        place, mine, other, (query_weight.shape, keys_first.shape, keys_second.shape)
    )
    return (mixed, token_grad, qw_grad, first_grad, second_grad, value_grad)


def solution(mesh):
    return jax.shard_map(
        body,
        mesh=mesh,
        in_specs=(
            P(("dp", "row"), "dim"),
            P("dim", None),
            P(),
            P(),
            P("row", "dim"),
            P(("dp", "row"), None),
            P(("dp", "row"), "dim"),
        ),
        out_specs=(
            P(("dp", "row"), "dim"),
            P(("dp", "row"), "dim"),
            P("dim", None),
            P(),
            P(),
            P(("row", "dp"), "dim"),
        ),
        check_vma=False,
    )
```

```python
import functools

import jax
import jax.numpy as jnp
from jax import lax
from jax.experimental import pallas as pl
from jax.experimental.pallas import tpu as pltpu
from jax.sharding import PartitionSpec as P

BF = jnp.bfloat16
F32 = jnp.float32
I32 = jnp.int32
NT = (((1,), (1,)), ((), ()))
TN = (((0,), (0,)), ((), ()))
MIB = 1 << 20


def dot(x, y, dims=(((1,), (0,)), ((), ()))):
    return lax.dot_general(x, y, dims, preferred_element_type=F32)


def iota(shape, dim):
    return lax.broadcasted_iota(I32, shape, dim)


def whole(shape):
    return pl.BlockSpec(shape, lambda *_: (0,) * len(shape))


def owner_order(picks, row_dev, n_z, n_x):
    owner = picks // row_dev
    return owner % n_z * n_x + owner // n_z


def small_iota(shape, dim):
    return iota(shape, dim).astype(F32).astype(BF)


def small(array):
    return array.astype(F32).astype(BF)


def hot_slots(slots, rank):
    topk, tok = rank.shape
    at_slot = small_iota((slots.shape[0], tok), 0)
    rank = small(rank)
    one, zero = jnp.ones((), BF), jnp.zeros((), BF)
    for at in range(topk):
        slots[:, at * tok : (at + 1) * tok] = jnp.where(at_slot == rank[at : at + 1, :], one, zero)


def place_kernel(row_dev, n_z, n_row, picks_ref, rank_ref):
    topk, tok = picks_ref.shape
    owner = owner_order(picks_ref[...], row_dev, n_z, n_row // n_z)
    at_owner = iota((n_row, tok), 0)
    onehots = [(at_owner == owner[k : k + 1, :]) for k in range(topk)]
    stacked = jnp.concatenate([jnp.where(hot, 1.0, 0.0) for hot in onehots], axis=0).astype(BF)
    upto = jnp.where(iota((tok, tok), 0) <= iota((tok, tok), 1), 1.0, 0.0).astype(BF)
    running = dot(stacked, upto)
    totals = dot(stacked, jnp.ones((tok, tok), BF))
    base = jnp.full((n_row, tok), -1.0, F32)
    for k in range(topk):
        part = slice(k * n_row, (k + 1) * n_row)
        rank = jnp.sum(jnp.where(onehots[k], running[part] + base, 0.0), axis=0, keepdims=True)
        base = base + totals[part]
        rank_ref[k : k + 1, :] = rank.astype(I32)


def place_picks(picks_t, row_dev, n_row, n_z):
    return pl.pallas_call(
        functools.partial(place_kernel, row_dev, n_z, n_row),
        out_shape=jax.ShapeDtypeStruct(picks_t.shape, I32),
        compiler_params=pltpu.CompilerParams(vmem_limit_bytes=12 * MIB),
        cost_estimate=pl.CostEstimate(flops=1_000_000_000, bytes_accessed=200_000, transcendentals=0),
        name="place_picks",
    )(picks_t)


def take_rows(table, index):
    topk, tok = index.shape
    within, group = index % 8, index // 8
    parts = [slice(q, q + 8) for q in range(0, topk, 8)]
    found = [jnp.zeros((8, tok), F32) for _ in parts]
    for g in range(table.shape[0] // 8):
        rows = table[8 * g : 8 * g + 8, :]
        for q, part in enumerate(parts):
            got = jnp.take_along_axis(rows, within[part], axis=0, mode="promise_in_bounds")
            found[q] = jnp.where(group[part] == g, got, found[q])
    return jnp.concatenate(found, axis=0)


def weigh_kernel(
    row_dev, n_x, query_ref, first_ref, second_ref, picks_ref, rank_ref, grad_ref,
    sent_ref, weight_ref, score_a, score_b, lhs, slots,
):
    topk, tok = picks_ref.shape
    half = first_ref.shape[1]
    nb = second_ref.shape[0]
    n_z = sent_ref.shape[0]
    query = query_ref[...]
    score_a[...] = dot(first_ref[...], query[:, :half], NT)
    score_b[...] = dot(second_ref[...], query[:, half:], NT)
    picks = picks_ref[...]
    score = take_rows(score_a, picks // nb) + take_rows(score_b, picks % nb)
    expo = jnp.exp(score)
    weight = expo / jnp.sum(expo, axis=0, keepdims=True)
    weight_ref[...] = weight
    weight = weight.astype(BF)
    local = picks % row_dev
    high, low = small(local // 256), small(local % 256)
    owner = small(owner_order(picks, row_dev, n_z, n_x))
    rows = (4 * n_z * n_x, tok)
    at_owner = small(iota(rows, 0) // 4)
    kind = small(iota(rows, 0) % 4)
    token = small_iota((1, tok), 1)
    zero = jnp.zeros((), BF)
    for k in range(topk):
        at = slice(k, k + 1)
        value = jnp.where(kind == 0.0, weight[at, :], jnp.where(
            kind == 1.0, high[at, :], jnp.where(kind == 2.0, low[at, :], token)))
        lhs[:, k * tok : (k + 1) * tok] = jnp.where(at_owner == owner[at, :], value, zero)
    hot_slots(slots, rank_ref[...])
    lists = dot(lhs[...], slots[...], NT).astype(BF)
    fold, cap = tok // 2, slots.shape[0]
    for z in range(n_z):
        sent_ref[z, :fold, :cap] = grad_ref[:fold]
        sent_ref[z, :fold, cap:] = grad_ref[fold:]
        sent_ref[z, fold:, :cap] = lists[4 * n_x * z : 4 * n_x * (z + 1)]
        sent_ref[z, fold:, cap:] = jnp.zeros((4 * n_x, cap), BF)


def weigh(query, keys_first, keys_second, picks_t, rank, out_grad, row_dev, n_x, n_z, cap):
    topk, tok = picks_t.shape
    cols = out_grad.shape[1]
    return pl.pallas_call(
        functools.partial(weigh_kernel, row_dev, n_x),
        out_shape=(
            jax.ShapeDtypeStruct((n_z, tok // 2 + 4 * n_x, 2 * cols), BF),
            jax.ShapeDtypeStruct((topk, tok), F32),
        ),
        scratch_shapes=[
            pltpu.VMEM((keys_first.shape[0], tok), F32),
            pltpu.VMEM((keys_second.shape[0], tok), F32),
            pltpu.VMEM((4 * n_x * n_z, topk * tok), BF),
            pltpu.VMEM((cap, topk * tok), BF),
        ],
        compiler_params=pltpu.CompilerParams(vmem_limit_bytes=12 * MIB),
        cost_estimate=pl.CostEstimate(flops=4_000_000_000, bytes_accessed=1_000_000, transcendentals=4096),
        name="weigh",
    )(query, keys_first, keys_second, picks_t, rank, out_grad)


def unfolded(got):
    rows, cols = got.shape[0] - 16, got.shape[1] // 2
    return jnp.concatenate([got[:rows, :cols], got[:rows, cols:]], axis=0)


def listed(lists, x_own, kind):
    return lists[pl.ds(4 * x_own + kind, 1), :]


def owner_kernel(place_ref, got_ref, *rest):
    n_x = (len(rest) - 6) // 2
    value_refs = rest[: 2 * n_x]
    mixed_ref, pick_ref, values, hot, lists, done = rest[2 * n_x :]
    cap = 2 * pick_ref.shape[2]
    half = value_refs[0].shape[0]
    rows = value_refs[0].shape[1]
    tok = mixed_ref.shape[0]
    x_at, dp_at = place_ref[0], place_ref[1]

    @pl.when(pl.program_id(0) == 0)
    def _():
        copies = []
        for i, ref in enumerate(value_refs):
            at = pl.multiple_of((dp_at if i % 2 == 0 else 1 - dp_at) * half, half)
            place = values.at[i // 2, pl.ds(at, half), :]
            copies.append(pltpu.make_async_copy(ref, place, done.at[i]))
        for copy in copies:
            copy.start()
        for copy in copies:
            copy.wait()

    lists[...] = got_ref[0, tok // 2 :, : lists.shape[1]].astype(F32)
    count = small_iota((256, cap), 0)
    one, zero = jnp.ones((), BF), jnp.zeros((), BF)
    picked = []
    weights = []
    tokens = []
    for s in range(n_x):
        x_own = lax.rem(x_at - s + n_x, n_x)
        weights.append(listed(lists, x_own, 0))
        tokens.append(listed(lists, x_own, 3))
        high, low = listed(lists, x_own, 1), listed(lists, x_own, 2)
        for at in range(rows // 256):
            here = jnp.where(high == at, low, -1.0).astype(BF)
            hot[s, at * 256 : (at + 1) * 256, :] = jnp.where(count == here, one, zero)
        picked.append(dot(values[s], hot[s]))
    picked = jnp.concatenate(picked, axis=1)
    token = jnp.concatenate(tokens, axis=1).astype(BF)
    weight = jnp.concatenate(weights, axis=1).astype(BF)
    at_token = small_iota((tok, n_x * cap), 0) == token
    spread = dot(unfolded(got_ref[0]), jnp.where(at_token, one, zero), TN)
    pick = jnp.sum(picked * spread, axis=0, keepdims=True)
    for s in range(n_x):
        x_own = lax.rem(x_at - s + n_x, n_x)
        for half_at in range(2):
            at = s * cap + half_at * 128
            pick_ref[0, pl.ds(2 * x_own + half_at, 1), :] = pick[:, at : at + 128]
    mixed_ref[...] = dot(jnp.where(at_token, weight, zero), picked.astype(BF), NT)


def owner_side(place, got, value_halves, cap):
    blocks, tall, cols = got.shape
    n_x = len(value_halves) // 2
    tok, width, cols = 2 * (tall - 4 * n_x), cols, cols // 2
    half, rows = value_halves[0].shape
    return pl.pallas_call(
        owner_kernel,
        grid_spec=pltpu.PrefetchScalarGridSpec(
            num_scalar_prefetch=1,
            grid=(blocks,),
            in_specs=[pl.BlockSpec((1, tall, width), lambda b, place: (b, 0, 0))]
            + [pl.BlockSpec(memory_space=pltpu.HBM)] * (2 * n_x),
            out_specs=[
                pl.BlockSpec((tok, cols), lambda b, place: (b, 0)),
                pl.BlockSpec((1, 2 * n_x, cap // 2), lambda b, place: (b, 0, 0)),
            ],
            scratch_shapes=[
                pltpu.VMEM((n_x, cols, rows), BF),
                pltpu.VMEM((n_x, rows, cap), BF),
                pltpu.VMEM((4 * n_x, cap), F32),
                pltpu.SemaphoreType.DMA((2 * n_x,)),
            ],
        ),
        out_shape=(
            jax.ShapeDtypeStruct((blocks * tok, cols), F32),
            jax.ShapeDtypeStruct((blocks, 2 * n_x, cap // 2), F32),
        ),
        compiler_params=pltpu.CompilerParams(vmem_limit_bytes=20 * MIB),
        cost_estimate=pl.CostEstimate(flops=12_000_000_000, bytes_accessed=10_000_000, transcendentals=0),
        name="owner_side",
    )(place, got, *value_halves)


def scatter_kernel(n_after, place_ref, got_ref, *rest):
    come_refs, (out_ref, hot, spread, lists) = rest[n_after:-4], rest[-4:]
    blocks, kinds, cap = lists.shape
    tok = 2 * (got_ref.shape[1] - kinds)
    x_own = place_ref[0]
    one, zero = jnp.ones((), BF), jnp.zeros((), BF)

    @pl.when(pl.program_id(0) == 0)
    def _():
        at_token = small_iota((tok, cap), 0)
        for at in range(blocks):
            lists[at] = got_ref[at, tok // 2 :, :cap].astype(F32)
            token = listed(lists.at[at], x_own, 3).astype(BF)
            spread[:, at * cap : (at + 1) * cap] = dot(
                unfolded(got_ref[at]), jnp.where(at_token == token, one, zero), TN
            ).astype(BF)

    chunk = (place_ref[2] * pl.num_programs(0) + pl.program_id(0)).astype(F32)
    count = small_iota((256, cap), 0)
    for at in range(blocks):
        weight = listed(lists.at[at], x_own, 0).astype(BF)
        high, low = listed(lists.at[at], x_own, 1), listed(lists.at[at], x_own, 2)
        here = jnp.where(high == chunk, low, -1.0).astype(BF)
        hot[:, at * cap : (at + 1) * cap] = jnp.where(count == here, weight, zero)
    total = dot(hot[...], spread[...], NT)
    for come_ref in come_refs:
        total = total + come_ref[...]
    out_ref[...] = total.astype(out_ref.dtype)


def scatter(place, got, after, rows, n_x, come=()):
    blocks, tall, width = got.shape
    cols = cap = width // 2
    half = rows // 2
    each = pl.BlockSpec((256, cols), lambda r, place: (r, 0))
    fixed = pl.BlockSpec(got.shape, lambda r, place: (0, 0, 0), pipeline_mode=pl.Buffered(1))
    return pl.pallas_call(
        functools.partial(scatter_kernel, len(after)),
        grid_spec=pltpu.PrefetchScalarGridSpec(
            num_scalar_prefetch=1,
            grid=(half // 256,),
            in_specs=[fixed] + [pl.BlockSpec(memory_space=pl.ANY)] * len(after) + [each] * len(come),
            out_specs=each,
            scratch_shapes=[
                pltpu.VMEM((256, blocks * cap), BF),
                pltpu.VMEM((cols, blocks * cap), BF),
                pltpu.VMEM((blocks, 4 * n_x, cap), F32),
            ],
        ),
        out_shape=jax.ShapeDtypeStruct((half, cols), F32),
        compiler_params=pltpu.CompilerParams(vmem_limit_bytes=16 * MIB),
        cost_estimate=pl.CostEstimate(flops=5_000_000_000, bytes_accessed=6_000_000, transcendentals=0),
        name="scatter_mine" if come else "scatter_theirs",
    )(place, got, *after, *come)


def grads_kernel(
    row_dev, n_z, place_ref, parts_ref, rank_ref, picks_ref, weight_ref, query_ref, first_ref, second_ref,
    qw_ref, tokens_ref, token_grad_ref, mine_ref, theirs_ref, slots, sums, grad_b, halves,
):
    topk, tok = picks_ref.shape
    half = first_ref.shape[1]
    na, nb = first_ref.shape[0], second_ref.shape[0]
    n_row, cap = parts_ref.shape[0] * parts_ref.shape[2] // 2, 2 * parts_ref.shape[3]
    halves[...] = jnp.sum(parts_ref[...], axis=1).reshape(2 * n_row, cap // 2)
    by_slot = jnp.concatenate(
        [halves[pl.ds(0, n_row, stride=2), :], halves[pl.ds(1, n_row, stride=2), :]], axis=1
    )
    one = by_slot.astype(BF)
    rest = by_slot - one.astype(F32)
    two = rest.astype(BF)
    three = (rest - two.astype(F32)).astype(BF)
    hot_slots(slots, rank_ref[...])
    sums[...] = dot(jnp.concatenate([one, two, three], axis=0), slots[...])
    picks = picks_ref[...]
    owner = owner_order(picks, row_dev, n_z, n_row // n_z)
    at_owner = iota((n_row, tok), 0)
    rows = []
    for k in range(topk):
        got = sums[:, k * tok : (k + 1) * tok]
        got = got[:n_row] + got[n_row : 2 * n_row] + got[2 * n_row :]
        rows.append(jnp.sum(jnp.where(at_owner == owner[k : k + 1, :], got, 0.0), axis=0, keepdims=True))
    pick_grad = jnp.concatenate(rows, axis=0)
    weight = weight_ref[...]
    score_grad = weight * (pick_grad - jnp.sum(weight * pick_grad, axis=0, keepdims=True))
    first_index = picks // nb
    second_index = picks % nb
    grad_a = jnp.zeros((na, tok), F32)
    for k in range(topk):
        grad_a = grad_a + jnp.where(
            iota((na, tok), 0) == first_index[k : k + 1, :], score_grad[k : k + 1, :], 0.0
        )
    grad_a = grad_a.astype(BF)
    tile = 128

    def one_tile(i, carry):
        at_b = iota((tile, tok), 0) + i * tile
        total = jnp.zeros((tile, tok), F32)
        for k in range(topk):
            total = total + jnp.where(
                at_b == second_index[k : k + 1, :], score_grad[k : k + 1, :], 0.0
            )
        grad_b[pl.ds(pl.multiple_of(i * tile, tile), tile), :] = total.astype(BF)
        return carry

    lax.fori_loop(0, nb // tile, one_tile, 0)
    query = query_ref[...]
    query_grad = jnp.concatenate(
        [dot(grad_a, first_ref[...], TN), dot(grad_b[...], second_ref[...], TN)], axis=1
    ).astype(BF)
    token_grad_ref[...] = dot(query_grad, qw_ref[...], NT).astype(BF)
    n_qw = tokens_ref.shape[1]
    at_second, end = n_qw + nb // 2, n_qw + (nb + na) // 2
    query_a, query_b = query[:, :half], query[:, half:]
    parts = []
    for h in range(2):
        qw_part = dot(query_grad[:, h * half : (h + 1) * half], tokens_ref[...], TN)
        own_b = slice(h * (nb // 2), (h + 1) * (nb // 2))
        second_part = dot(query_b, grad_b[own_b, :], (((0,), (1,)), ((), ())))
        first_part = dot(query_a, grad_a[h * (na // 2) : (h + 1) * (na // 2)], (((0,), (1,)), ((), ())))
        rest = jnp.zeros((half, mine_ref.shape[1] - end), F32)
        parts.append(jnp.concatenate([qw_part, second_part, first_part, rest], axis=1))
    swap = place_ref[1] == 1
    mine_ref[...] = jnp.where(swap, parts[1], parts[0])
    theirs_ref[...] = jnp.where(swap, parts[0], parts[1]).astype(theirs_ref.dtype)


def grads(place, parts, rank, picks_t, weight, query, keys_first, keys_second, qw, tokens, row_dev, n_z):
    topk, tok = picks_t.shape
    cap = 2 * parts.shape[3]
    n_row = parts.shape[0] * parts.shape[2] // 2
    na, half = keys_first.shape
    nb = keys_second.shape[0]
    folded = (half, -(-(qw.shape[0] + (na + nb) // 2) // 128) * 128)
    return pl.pallas_call(
        functools.partial(grads_kernel, row_dev, n_z),
        in_specs=[pl.BlockSpec(memory_space=pltpu.SMEM)] + [pl.BlockSpec(memory_space=pltpu.VMEM)] * 9,
        out_shape=(
            jax.ShapeDtypeStruct(tokens.shape, BF),
            jax.ShapeDtypeStruct(folded, F32),
            jax.ShapeDtypeStruct(folded, BF),
        ),
        scratch_shapes=[
            pltpu.VMEM((cap, topk * tok), BF),
            pltpu.VMEM((3 * n_row, topk * tok), F32),
            pltpu.VMEM((nb, tok), BF),
            pltpu.VMEM((2 * n_row, cap // 2), F32),
        ],
        compiler_params=pltpu.CompilerParams(vmem_limit_bytes=16 * MIB),
        cost_estimate=pl.CostEstimate(flops=4_000_000_000, bytes_accessed=4_000_000, transcendentals=0),
        name="grads",
    )(place, parts, rank, picks_t, weight, query, keys_first, keys_second, qw, tokens)


def unfold_kernel(place_ref, mine_ref, other_ref, qw_ref, first_ref, second_ref):
    n_qw, n_second, n_first = qw_ref.shape[0], second_ref.shape[0] // 2, first_ref.shape[0] // 2
    half = mine_ref.shape[0]
    for side, ref in ((place_ref[1], mine_ref), (place_ref[2], other_ref)):
        qw_ref[:, pl.ds(pl.multiple_of(side * half, half), half)] = ref[:, :n_qw].astype(F32).T
        second_ref[pl.ds(pl.multiple_of(side * n_second, n_second), n_second), :] = (
            ref[:, n_qw : n_qw + n_second].astype(F32).T
        )
        first_ref[pl.ds(pl.multiple_of(side * n_first, n_first), n_first), :] = (
            ref[:, n_qw + n_second : n_qw + n_second + n_first].astype(F32).T
        )


def unfold(place, mine, other, shapes):
    return pl.pallas_call(
        unfold_kernel,
        in_specs=[pl.BlockSpec(memory_space=pltpu.SMEM)] + [pl.BlockSpec(memory_space=pltpu.VMEM)] * 2,
        out_shape=tuple(jax.ShapeDtypeStruct(shape, F32) for shape in shapes),
        compiler_params=pltpu.CompilerParams(vmem_limit_bytes=12 * MIB),
        name="unfold",
    )(place, mine, other)


def body(tokens, query_weight, keys_first, keys_second, values, picks, out_grad):
    tok, topk = picks.shape
    row_dev, cols = values.shape
    na, half = keys_first.shape
    nb = keys_second.shape[0]
    n_row, n_dim = lax.axis_size("row"), lax.axis_size("dim")
    cap = 2 * tok * topk // n_row
    n_x = 4
    n_z = n_row // n_x
    row_at, dp_at = lax.axis_index("row"), lax.axis_index("dp")
    place = jnp.stack([row_at // n_z, dp_at, 1 - dp_at, row_at % n_z]).astype(I32)
    rings = [[x * n_z + z for z in range(n_z)] for x in range(n_x)]
    columns = [[x * n_z + z for x in range(n_x)] for z in range(n_z)]
    planes = [[r * n_dim + m for r in ring for m in range(n_dim)] for ring in rings]

    def other_core(array):
        return lax.ppermute(array, "dp", [(0, 1), (1, 0)])

    def along_x(array, shift):
        pairs = [(x * n_z + z, (x + shift) % n_x * n_z + z) for x in range(n_x) for z in range(n_z)]
        return lax.ppermute(array, "row", pairs)

    def along_dim(array, shift):
        return lax.ppermute(array, "dim", [(m, (m + shift) % n_dim) for m in range(n_dim)])

    partial = dot(tokens, query_weight)
    partial, values = lax.optimization_barrier((partial, values))
    near = [along_dim(partial, s) for s in (1, 2, 3)]
    picks_t = picks.T
    rank = place_picks(picks_t, row_dev, n_row, n_z)

    values_t = values.T
    own_half = lax.dynamic_slice_in_dim(values_t, dp_at * (cols // 2), cols // 2, 0)
    other_half = lax.dynamic_slice_in_dim(values_t, (1 - dp_at) * (cols // 2), cols // 2, 0)
    value_halves = [own_half, other_half]
    for s in range(1, n_x):
        got = along_x(own_half, s)
        value_halves += [got, other_core(got)]

    query = ((partial + near[1]) + (near[0] + near[2])).astype(BF)
    query, rank = lax.optimization_barrier((query, rank))
    sent, weight = weigh(
        query, keys_first, keys_second, picks_t, rank, out_grad, row_dev, n_x, n_z, cap
    )
    got = lax.all_to_all(sent, "row", 0, 0, tiled=True, axis_index_groups=rings)

    corners = [part[:8, :128] for part in value_halves[3::2]]
    late, corners = lax.optimization_barrier((got, corners))
    got_x = lax.all_gather(late, "row", tiled=True, axis_index_groups=columns)
    mixed_part, pick_part = owner_side(place, got, value_halves, cap)
    pick_sent = jnp.broadcast_to(pick_part[:, None], (n_z, n_dim) + pick_part.shape[1:])
    pick_parts = lax.all_to_all(
        pick_sent.reshape((n_z * n_dim,) + pick_part.shape[1:]), ("row", "dim"), 0, 0, tiled=True,
        axis_index_groups=planes,
    ).reshape(pick_sent.shape)

    mixed = lax.psum_scatter(
        mixed_part, "row", tiled=True, axis_index_groups=rings
    ).astype(BF)
    token_grad, mine, theirs = grads(
        place, pick_parts, rank, picks_t, weight, query, keys_first, keys_second, query_weight, tokens,
        row_dev, n_z,
    )
    mine = (mine + other_core(theirs).astype(F32)).astype(BF)
    shape = (n_row, half // n_row, mine.shape[1])
    received = lax.all_to_all(mine.reshape(shape), "row", 0, 0, tiled=True)
    summed = jnp.sum(received.astype(F32), axis=0).astype(BF)
    come = other_core(scatter(place, got_x, corners, row_dev, n_x))
    summed, come = lax.optimization_barrier((summed, come))
    summed = jnp.broadcast_to(summed[None], shape)
    mine = lax.all_to_all(summed, "row", 0, 0, tiled=True).reshape(mine.shape)
    own_place = jnp.stack([row_at // n_z, dp_at, dp_at]).astype(I32)
    value_grad = scatter(own_place, got_x, corners, row_dev, n_x, (come,))
    mine, mixed, value_grad = lax.optimization_barrier((mine, mixed, value_grad))
    other = other_core(mine)
    qw_grad, first_grad, second_grad = unfold(
        place, mine, other, (query_weight.shape, keys_first.shape, keys_second.shape)
    )
    return (mixed, token_grad, qw_grad, first_grad, second_grad, value_grad)


def solution(mesh):
    return jax.shard_map(
        body,
        mesh=mesh,
        in_specs=(
            P(("dp", "row"), "dim"),
            P("dim", None),
            P(),
            P(),
            P("row", "dim"),
            P(("dp", "row"), None),
            P(("dp", "row"), "dim"),
        ),
        out_specs=(
            P(("dp", "row"), "dim"),
            P(("dp", "row"), "dim"),
            P("dim", None),
            P(),
            P(),
            P(("row", "dp"), "dim"),
        ),
        check_vma=False,
    )
```

```python
import functools

import jax
import jax.numpy as jnp
from jax import lax
from jax.experimental import pallas as pl
from jax.experimental.pallas import tpu as pltpu
from jax.sharding import PartitionSpec as P

BF = jnp.bfloat16
F32 = jnp.float32
I32 = jnp.int32
NT = (((1,), (1,)), ((), ()))
TN = (((0,), (0,)), ((), ()))
MIB = 1 << 20


def dot(x, y, dims=(((1,), (0,)), ((), ()))):
    return lax.dot_general(x, y, dims, preferred_element_type=F32)


def iota(shape, dim):
    return lax.broadcasted_iota(I32, shape, dim)


def whole(shape):
    return pl.BlockSpec(shape, lambda *_: (0,) * len(shape))


def owner_order(picks, row_dev, n_z, n_x):
    owner = picks // row_dev
    return owner % n_z * n_x + owner // n_z


def small_iota(shape, dim):
    return iota(shape, dim).astype(F32).astype(BF)


def small(array):
    return array.astype(F32).astype(BF)


def hot_slots(slots, rank):
    topk, tok = rank.shape
    at_slot = small_iota((slots.shape[0], tok), 0)
    rank = small(rank)
    one, zero = jnp.ones((), BF), jnp.zeros((), BF)
    for at in range(topk):
        slots[:, at * tok : (at + 1) * tok] = jnp.where(at_slot == rank[at : at + 1, :], one, zero)


def place_kernel(row_dev, n_z, n_row, picks_ref, rank_ref):
    topk, tok = picks_ref.shape
    owner = owner_order(picks_ref[...], row_dev, n_z, n_row // n_z)
    at_owner = iota((n_row, tok), 0)
    onehots = [(at_owner == owner[k : k + 1, :]) for k in range(topk)]
    stacked = jnp.concatenate([jnp.where(hot, 1.0, 0.0) for hot in onehots], axis=0).astype(BF)
    upto = jnp.where(iota((tok, tok), 0) <= iota((tok, tok), 1), 1.0, 0.0).astype(BF)
    running = dot(stacked, upto)
    totals = dot(stacked, jnp.ones((tok, tok), BF))
    base = jnp.full((n_row, tok), -1.0, F32)
    for k in range(topk):
        part = slice(k * n_row, (k + 1) * n_row)
        rank = jnp.sum(jnp.where(onehots[k], running[part] + base, 0.0), axis=0, keepdims=True)
        base = base + totals[part]
        rank_ref[k : k + 1, :] = rank.astype(I32)


def place_picks(picks_t, row_dev, n_row, n_z):
    return pl.pallas_call(
        functools.partial(place_kernel, row_dev, n_z, n_row),
        out_shape=jax.ShapeDtypeStruct(picks_t.shape, I32),
        compiler_params=pltpu.CompilerParams(vmem_limit_bytes=12 * MIB),
        cost_estimate=pl.CostEstimate(flops=1_000_000_000, bytes_accessed=200_000, transcendentals=0),
        name="place_picks",
    )(picks_t)


def take_rows(table, index):
    topk, tok = index.shape
    within, group = index % 8, index // 8
    parts = [slice(q, q + 8) for q in range(0, topk, 8)]
    found = [jnp.zeros((8, tok), F32) for _ in parts]
    for g in range(table.shape[0] // 8):
        rows = table[8 * g : 8 * g + 8, :]
        for q, part in enumerate(parts):
            got = jnp.take_along_axis(rows, within[part], axis=0, mode="promise_in_bounds")
            found[q] = jnp.where(group[part] == g, got, found[q])
    return jnp.concatenate(found, axis=0)


def weigh_kernel(
    row_dev, n_x, query_ref, first_ref, second_ref, picks_ref, rank_ref, grad_ref,
    sent_ref, weight_ref, score_a, score_b, lhs, slots,
):
    topk, tok = picks_ref.shape
    half = first_ref.shape[1]
    nb = second_ref.shape[0]
    n_z = sent_ref.shape[0]
    query = query_ref[...]
    score_a[...] = dot(first_ref[...], query[:, :half], NT)
    score_b[...] = dot(second_ref[...], query[:, half:], NT)
    picks = picks_ref[...]
    score = take_rows(score_a, picks // nb) + take_rows(score_b, picks % nb)
    expo = jnp.exp(score)
    weight = expo / jnp.sum(expo, axis=0, keepdims=True)
    weight_ref[...] = weight
    weight = weight.astype(BF)
    local = picks % row_dev
    high, low = small(local // 256), small(local % 256)
    owner = small(owner_order(picks, row_dev, n_z, n_x))
    rows = (4 * n_z * n_x, tok)
    at_owner = small(iota(rows, 0) // 4)
    kind = small(iota(rows, 0) % 4)
    token = small_iota((1, tok), 1)
    zero = jnp.zeros((), BF)
    for k in range(topk):
        at = slice(k, k + 1)
        value = jnp.where(kind == 0.0, weight[at, :], jnp.where(
            kind == 1.0, high[at, :], jnp.where(kind == 2.0, low[at, :], token)))
        lhs[:, k * tok : (k + 1) * tok] = jnp.where(at_owner == owner[at, :], value, zero)
    hot_slots(slots, rank_ref[...])
    lists = dot(lhs[...], slots[...], NT).astype(BF)
    for z in range(n_z):
        sent_ref[z, :tok, :] = grad_ref[...]
        sent_ref[z, tok:, :] = lists[4 * n_x * z : 4 * n_x * (z + 1)]


def weigh(query, keys_first, keys_second, picks_t, rank, out_grad, row_dev, n_x, n_z, cap):
    topk, tok = picks_t.shape
    cols = out_grad.shape[1]
    return pl.pallas_call(
        functools.partial(weigh_kernel, row_dev, n_x),
        out_shape=(
            jax.ShapeDtypeStruct((n_z, tok + 4 * n_x, cols), BF),
            jax.ShapeDtypeStruct((topk, tok), F32),
        ),
        scratch_shapes=[
            pltpu.VMEM((keys_first.shape[0], tok), F32),
            pltpu.VMEM((keys_second.shape[0], tok), F32),
            pltpu.VMEM((4 * n_x * n_z, topk * tok), BF),
            pltpu.VMEM((cap, topk * tok), BF),
        ],
        compiler_params=pltpu.CompilerParams(vmem_limit_bytes=12 * MIB),
        cost_estimate=pl.CostEstimate(flops=4_000_000_000, bytes_accessed=1_000_000, transcendentals=4096),
        name="weigh",
    )(query, keys_first, keys_second, picks_t, rank, out_grad)


def listed(lists, x_own, kind):
    return lists[pl.ds(4 * x_own + kind, 1), :]


def owner_kernel(place_ref, got_ref, *rest):
    n_x = (len(rest) - 6) // 2
    value_refs = rest[: 2 * n_x]
    mixed_ref, pick_ref, values, hot, lists, done = rest[2 * n_x :]
    cap = 2 * pick_ref.shape[2]
    half = value_refs[0].shape[0]
    rows = value_refs[0].shape[1]
    tok = mixed_ref.shape[0]
    x_at, dp_at = place_ref[0], place_ref[1]

    @pl.when(pl.program_id(0) == 0)
    def _():
        copies = []
        for i, ref in enumerate(value_refs):
            at = pl.multiple_of((dp_at if i % 2 == 0 else 1 - dp_at) * half, half)
            place = values.at[i // 2, pl.ds(at, half), :]
            copies.append(pltpu.make_async_copy(ref, place, done.at[i]))
        for copy in copies:
            copy.start()
        for copy in copies:
            copy.wait()

    lists[...] = got_ref[0, tok:, :].astype(F32)
    count = small_iota((256, cap), 0)
    one, zero = jnp.ones((), BF), jnp.zeros((), BF)
    picked = []
    weights = []
    tokens = []
    for s in range(n_x):
        x_own = lax.rem(x_at - s + n_x, n_x)
        weights.append(listed(lists, x_own, 0))
        tokens.append(listed(lists, x_own, 3))
        high, low = listed(lists, x_own, 1), listed(lists, x_own, 2)
        for at in range(rows // 256):
            here = jnp.where(high == at, low, -1.0).astype(BF)
            hot[s, at * 256 : (at + 1) * 256, :] = jnp.where(count == here, one, zero)
        picked.append(dot(values[s], hot[s]))
    picked = jnp.concatenate(picked, axis=1)
    token = jnp.concatenate(tokens, axis=1).astype(BF)
    weight = jnp.concatenate(weights, axis=1).astype(BF)
    at_token = small_iota((tok, n_x * cap), 0) == token
    spread = dot(got_ref[0, :tok, :], jnp.where(at_token, one, zero), TN)
    pick = jnp.sum(picked * spread, axis=0, keepdims=True)
    for s in range(n_x):
        x_own = lax.rem(x_at - s + n_x, n_x)
        for half_at in range(2):
            at = s * cap + half_at * 128
            pick_ref[0, pl.ds(2 * x_own + half_at, 1), :] = pick[:, at : at + 128]
    mixed_ref[...] = dot(jnp.where(at_token, weight, zero), picked.astype(BF), NT)


def owner_side(place, got, value_halves, cap):
    blocks, tall, cols = got.shape
    n_x = len(value_halves) // 2
    tok = tall - 4 * n_x
    half, rows = value_halves[0].shape
    return pl.pallas_call(
        owner_kernel,
        grid_spec=pltpu.PrefetchScalarGridSpec(
            num_scalar_prefetch=1,
            grid=(blocks,),
            in_specs=[pl.BlockSpec((1, tall, cols), lambda b, place: (b, 0, 0))]
            + [pl.BlockSpec(memory_space=pltpu.HBM)] * (2 * n_x),
            out_specs=[
                pl.BlockSpec((tok, cols), lambda b, place: (b, 0)),
                pl.BlockSpec((1, 2 * n_x, cap // 2), lambda b, place: (b, 0, 0)),
            ],
            scratch_shapes=[
                pltpu.VMEM((n_x, cols, rows), BF),
                pltpu.VMEM((n_x, rows, cap), BF),
                pltpu.VMEM((4 * n_x, cap), F32),
                pltpu.SemaphoreType.DMA((2 * n_x,)),
            ],
        ),
        out_shape=(
            jax.ShapeDtypeStruct((blocks * tok, cols), F32),
            jax.ShapeDtypeStruct((blocks, 2 * n_x, cap // 2), F32),
        ),
        compiler_params=pltpu.CompilerParams(vmem_limit_bytes=20 * MIB),
        cost_estimate=pl.CostEstimate(flops=12_000_000_000, bytes_accessed=10_000_000, transcendentals=0),
        name="owner_side",
    )(place, got, *value_halves)


def scatter_kernel(n_after, place_ref, got_ref, *rest):
    come_refs, (out_ref, hot, spread, lists) = rest[n_after:-4], rest[-4:]
    blocks, kinds, cap = lists.shape
    tok = got_ref.shape[1] - kinds
    x_own = place_ref[0]
    one, zero = jnp.ones((), BF), jnp.zeros((), BF)

    @pl.when(pl.program_id(0) == 0)
    def _():
        at_token = small_iota((tok, cap), 0)
        for at in range(blocks):
            lists[at] = got_ref[at, tok:, :].astype(F32)
            token = listed(lists.at[at], x_own, 3).astype(BF)
            spread[:, at * cap : (at + 1) * cap] = dot(
                got_ref[at, :tok, :], jnp.where(at_token == token, one, zero), TN
            ).astype(BF)

    chunk = (place_ref[2] * pl.num_programs(0) + pl.program_id(0)).astype(F32)
    count = small_iota((256, cap), 0)
    for at in range(blocks):
        weight = listed(lists.at[at], x_own, 0).astype(BF)
        high, low = listed(lists.at[at], x_own, 1), listed(lists.at[at], x_own, 2)
        here = jnp.where(high == chunk, low, -1.0).astype(BF)
        hot[:, at * cap : (at + 1) * cap] = jnp.where(count == here, weight, zero)
    total = dot(hot[...], spread[...], NT)
    for come_ref in come_refs:
        total = total + come_ref[...]
    out_ref[...] = total.astype(out_ref.dtype)


def scatter(place, got, after, rows, n_x, come=()):
    blocks, tall, cols = got.shape
    cap = cols
    half = rows // 2
    each = pl.BlockSpec((256, cols), lambda r, place: (r, 0))
    fixed = pl.BlockSpec(got.shape, lambda r, place: (0, 0, 0), pipeline_mode=pl.Buffered(1))
    return pl.pallas_call(
        functools.partial(scatter_kernel, len(after)),
        grid_spec=pltpu.PrefetchScalarGridSpec(
            num_scalar_prefetch=1,
            grid=(half // 256,),
            in_specs=[fixed] + [pl.BlockSpec(memory_space=pl.ANY)] * len(after) + [each] * len(come),
            out_specs=each,
            scratch_shapes=[
                pltpu.VMEM((256, blocks * cap), BF),
                pltpu.VMEM((cols, blocks * cap), BF),
                pltpu.VMEM((blocks, 4 * n_x, cap), F32),
            ],
        ),
        out_shape=jax.ShapeDtypeStruct((half, cols), F32),
        compiler_params=pltpu.CompilerParams(vmem_limit_bytes=16 * MIB),
        cost_estimate=pl.CostEstimate(flops=5_000_000_000, bytes_accessed=6_000_000, transcendentals=0),
        name="scatter_mine" if come else "scatter_theirs",
    )(place, got, *after, *come)


def grads_kernel(
    row_dev, n_z, place_ref, parts_ref, rank_ref, picks_ref, weight_ref, query_ref, first_ref, second_ref,
    qw_ref, tokens_ref, token_grad_ref, mine_ref, theirs_ref, slots, sums, grad_b, halves,
):
    topk, tok = picks_ref.shape
    half = first_ref.shape[1]
    na, nb = first_ref.shape[0], second_ref.shape[0]
    n_row, cap = parts_ref.shape[0] * parts_ref.shape[2] // 2, 2 * parts_ref.shape[3]
    halves[...] = jnp.sum(parts_ref[...], axis=1).reshape(2 * n_row, cap // 2)
    by_slot = jnp.concatenate(
        [halves[pl.ds(0, n_row, stride=2), :], halves[pl.ds(1, n_row, stride=2), :]], axis=1
    )
    one = by_slot.astype(BF)
    rest = by_slot - one.astype(F32)
    two = rest.astype(BF)
    three = (rest - two.astype(F32)).astype(BF)
    hot_slots(slots, rank_ref[...])
    sums[...] = dot(jnp.concatenate([one, two, three], axis=0), slots[...])
    picks = picks_ref[...]
    owner = owner_order(picks, row_dev, n_z, n_row // n_z)
    at_owner = iota((n_row, tok), 0)
    rows = []
    for k in range(topk):
        got = sums[:, k * tok : (k + 1) * tok]
        got = got[:n_row] + got[n_row : 2 * n_row] + got[2 * n_row :]
        rows.append(jnp.sum(jnp.where(at_owner == owner[k : k + 1, :], got, 0.0), axis=0, keepdims=True))
    pick_grad = jnp.concatenate(rows, axis=0)
    weight = weight_ref[...]
    score_grad = weight * (pick_grad - jnp.sum(weight * pick_grad, axis=0, keepdims=True))
    first_index = picks // nb
    second_index = picks % nb
    grad_a = jnp.zeros((na, tok), F32)
    for k in range(topk):
        grad_a = grad_a + jnp.where(
            iota((na, tok), 0) == first_index[k : k + 1, :], score_grad[k : k + 1, :], 0.0
        )
    grad_a = grad_a.astype(BF)
    tile = 128

    def one_tile(i, carry):
        at_b = iota((tile, tok), 0) + i * tile
        total = jnp.zeros((tile, tok), F32)
        for k in range(topk):
            total = total + jnp.where(
                at_b == second_index[k : k + 1, :], score_grad[k : k + 1, :], 0.0
            )
        grad_b[pl.ds(pl.multiple_of(i * tile, tile), tile), :] = total.astype(BF)
        return carry

    lax.fori_loop(0, nb // tile, one_tile, 0)
    query = query_ref[...]
    query_grad = jnp.concatenate(
        [dot(grad_a, first_ref[...], TN), dot(grad_b[...], second_ref[...], TN)], axis=1
    ).astype(BF)
    token_grad_ref[...] = dot(query_grad, qw_ref[...], NT).astype(BF)
    n_qw = tokens_ref.shape[1]
    at_second, end = n_qw + nb // 2, n_qw + (nb + na) // 2
    query_a, query_b = query[:, :half], query[:, half:]
    parts = []
    for h in range(2):
        qw_part = dot(query_grad[:, h * half : (h + 1) * half], tokens_ref[...], TN)
        own_b = slice(h * (nb // 2), (h + 1) * (nb // 2))
        second_part = dot(query_b, grad_b[own_b, :], (((0,), (1,)), ((), ())))
        first_part = dot(query_a, grad_a[h * (na // 2) : (h + 1) * (na // 2)], (((0,), (1,)), ((), ())))
        rest = jnp.zeros((half, mine_ref.shape[1] - end), F32)
        parts.append(jnp.concatenate([qw_part, second_part, first_part, rest], axis=1))
    swap = place_ref[1] == 1
    mine_ref[...] = jnp.where(swap, parts[1], parts[0])
    theirs_ref[...] = jnp.where(swap, parts[0], parts[1]).astype(theirs_ref.dtype)


def grads(place, parts, rank, picks_t, weight, query, keys_first, keys_second, qw, tokens, row_dev, n_z):
    topk, tok = picks_t.shape
    cap = 2 * parts.shape[3]
    n_row = parts.shape[0] * parts.shape[2] // 2
    na, half = keys_first.shape
    nb = keys_second.shape[0]
    folded = (half, -(-(qw.shape[0] + (na + nb) // 2) // 128) * 128)
    return pl.pallas_call(
        functools.partial(grads_kernel, row_dev, n_z),
        in_specs=[pl.BlockSpec(memory_space=pltpu.SMEM)] + [pl.BlockSpec(memory_space=pltpu.VMEM)] * 9,
        out_shape=(
            jax.ShapeDtypeStruct(tokens.shape, BF),
            jax.ShapeDtypeStruct(folded, F32),
            jax.ShapeDtypeStruct(folded, BF),
        ),
        scratch_shapes=[
            pltpu.VMEM((cap, topk * tok), BF),
            pltpu.VMEM((3 * n_row, topk * tok), F32),
            pltpu.VMEM((nb, tok), BF),
            pltpu.VMEM((2 * n_row, cap // 2), F32),
        ],
        compiler_params=pltpu.CompilerParams(vmem_limit_bytes=16 * MIB),
        cost_estimate=pl.CostEstimate(flops=4_000_000_000, bytes_accessed=4_000_000, transcendentals=0),
        name="grads",
    )(place, parts, rank, picks_t, weight, query, keys_first, keys_second, qw, tokens)


def unfold_kernel(place_ref, mine_ref, other_ref, qw_ref, first_ref, second_ref):
    n_qw, n_second, n_first = qw_ref.shape[0], second_ref.shape[0] // 2, first_ref.shape[0] // 2
    half = mine_ref.shape[0]
    for side, ref in ((place_ref[1], mine_ref), (place_ref[2], other_ref)):
        qw_ref[:, pl.ds(pl.multiple_of(side * half, half), half)] = ref[:, :n_qw].astype(F32).T
        second_ref[pl.ds(pl.multiple_of(side * n_second, n_second), n_second), :] = (
            ref[:, n_qw : n_qw + n_second].astype(F32).T
        )
        first_ref[pl.ds(pl.multiple_of(side * n_first, n_first), n_first), :] = (
            ref[:, n_qw + n_second : n_qw + n_second + n_first].astype(F32).T
        )


def unfold(place, mine, other, shapes):
    return pl.pallas_call(
        unfold_kernel,
        in_specs=[pl.BlockSpec(memory_space=pltpu.SMEM)] + [pl.BlockSpec(memory_space=pltpu.VMEM)] * 2,
        out_shape=tuple(jax.ShapeDtypeStruct(shape, F32) for shape in shapes),
        compiler_params=pltpu.CompilerParams(vmem_limit_bytes=12 * MIB),
        name="unfold",
    )(place, mine, other)


def body(tokens, query_weight, keys_first, keys_second, values, picks, out_grad):
    tok, topk = picks.shape
    row_dev, cols = values.shape
    na, half = keys_first.shape
    nb = keys_second.shape[0]
    n_row, n_dim = lax.axis_size("row"), lax.axis_size("dim")
    cap = 2 * tok * topk // n_row
    n_x = 4
    n_z = n_row // n_x
    row_at, dp_at = lax.axis_index("row"), lax.axis_index("dp")
    place = jnp.stack([row_at // n_z, dp_at, 1 - dp_at, row_at % n_z]).astype(I32)
    rings = [[x * n_z + z for z in range(n_z)] for x in range(n_x)]
    columns = [[x * n_z + z for x in range(n_x)] for z in range(n_z)]
    planes = [[r * n_dim + m for r in ring for m in range(n_dim)] for ring in rings]

    def other_core(array):
        return lax.ppermute(array, "dp", [(0, 1), (1, 0)])

    def along_x(array, shift):
        pairs = [(x * n_z + z, (x + shift) % n_x * n_z + z) for x in range(n_x) for z in range(n_z)]
        return lax.ppermute(array, "row", pairs)

    def along_dim(array, shift):
        return lax.ppermute(array, "dim", [(m, (m + shift) % n_dim) for m in range(n_dim)])

    partial = dot(tokens, query_weight)
    partial, values = lax.optimization_barrier((partial, values))
    near = [along_dim(partial, s) for s in (1, 2, 3)]
    picks_t = picks.T
    rank = place_picks(picks_t, row_dev, n_row, n_z)

    values_t = values.T
    own_half = lax.dynamic_slice_in_dim(values_t, dp_at * (cols // 2), cols // 2, 0)
    other_half = lax.dynamic_slice_in_dim(values_t, (1 - dp_at) * (cols // 2), cols // 2, 0)
    value_halves = [own_half, other_half]
    for s in range(1, n_x):
        got = along_x(own_half, s)
        value_halves += [got, other_core(got)]

    query = ((partial + near[1]) + (near[0] + near[2])).astype(BF)
    query, rank = lax.optimization_barrier((query, rank))
    sent, weight = weigh(
        query, keys_first, keys_second, picks_t, rank, out_grad, row_dev, n_x, n_z, cap
    )
    got = lax.all_to_all(sent, "row", 0, 0, tiled=True, axis_index_groups=rings)

    corners = [part[:8, :128] for part in value_halves[3::2]]
    late, corners = lax.optimization_barrier((got, corners))
    got_x = lax.all_gather(late, "row", tiled=True, axis_index_groups=columns)
    mixed_part, pick_part = owner_side(place, got, value_halves, cap)
    pick_sent = jnp.broadcast_to(pick_part[:, None], (n_z, n_dim) + pick_part.shape[1:])
    pick_parts = lax.all_to_all(
        pick_sent.reshape((n_z * n_dim,) + pick_part.shape[1:]), ("row", "dim"), 0, 0, tiled=True,
        axis_index_groups=planes,
    ).reshape(pick_sent.shape)

    token_grad, mine, theirs = grads(
        place, pick_parts, rank, picks_t, weight, query, keys_first, keys_second, query_weight, tokens,
        row_dev, n_z,
    )
    mine = (mine + other_core(theirs).astype(F32)).astype(BF)
    mine, mixed_part = lax.optimization_barrier((mine, mixed_part))
    mixed = lax.psum_scatter(
        mixed_part, "row", tiled=True, axis_index_groups=rings
    ).astype(BF)
    shape = (n_row, half // n_row, mine.shape[1])
    received = lax.all_to_all(mine.reshape(shape), "row", 0, 0, tiled=True)
    summed = jnp.sum(received.astype(F32), axis=0).astype(BF)
    come = other_core(scatter(place, got_x, corners, row_dev, n_x))
    summed, come = lax.optimization_barrier((summed, come))
    summed = jnp.broadcast_to(summed[None], shape)
    mine = lax.all_to_all(summed, "row", 0, 0, tiled=True).reshape(mine.shape)
    own_place = jnp.stack([row_at // n_z, dp_at, dp_at]).astype(I32)
    value_grad = scatter(own_place, got_x, corners, row_dev, n_x, (come,))
    mine, value_grad = lax.optimization_barrier((mine, value_grad))
    other = other_core(mine)
    qw_grad, first_grad, second_grad = unfold(
        place, mine, other, (query_weight.shape, keys_first.shape, keys_second.shape)
    )
    return (mixed, token_grad, qw_grad, first_grad, second_grad, value_grad)


def solution(mesh):
    return jax.shard_map(
        body,
        mesh=mesh,
        in_specs=(
            P(("dp", "row"), "dim"),
            P("dim", None),
            P(),
            P(),
            P("row", "dim"),
            P(("dp", "row"), None),
            P(("dp", "row"), "dim"),
        ),
        out_specs=(
            P(("dp", "row"), "dim"),
            P(("dp", "row"), "dim"),
            P("dim", None),
            P(),
            P(),
            P(("row", "dp"), "dim"),
        ),
        check_vma=False,
    )
```
